32 devices in a mesh: dp: 4 (over y, x), fsdp: 8 (over z, core).
Axes of the slice: x: 2, y: 2, z: 4, core: 2. Of those that a mesh axis runs over, the one named last changes fastest.
Arguments:
- tokens: bfloat16 [64, 128, 768], P(('dp', 'fsdp')), may hold values from -6 to 6
- lengths: int32 [64], P(('dp', 'fsdp')), may hold values from 1 to 128, as said below
- timesteps: int32 [64], P(('dp', 'fsdp')), may hold values from 0 to 1999
- cotangent: bfloat16 [64, 128, 768], P(('dp', 'fsdp')), may hold values from -6 to 6
- params: float32 [7547136], P('fsdp')
- moment_one: float32 [7547136], P('fsdp')
- moment_two: float32 [7547136], P('fsdp')
Outputs:
- output: bfloat16 [64, 128, 768], P(('dp', 'fsdp'))
- token_grad: float32 [64, 128, 768], P(('dp', 'fsdp'))
- new_params: float32 [7547136], P('fsdp')
- new_moment_one: float32 [7547136], P('fsdp')
- new_moment_two: float32 [7547136], P('fsdp')
The draws below stay inside these ranges and needn't reach their ends.
Inputs may be any that keep to these rules, and one draw needn't show every extreme that they name: `lengths`: padding follows each sequence's length; some sequence has length 128 in every draw.
All inputs are finite; a program needn't handle non-finite values.
Results may differ from the reference program's by a relative error of at most 0.013.
The reference program's roundings to bfloat16 on the way count: a program that leaves them out, or rounds other values in their place, can miss the bound.
Values may be sent and summed in bfloat16 or wider, within the bound.
No kernel may reach another device: no remote copies, remote signals or barrier semaphores. Data moves between devices by JAX's collectives and lax.ppermute only.
A program may use at most 192 MiB of HBM per device.

```python
import math
import jax
import jax.numpy as jnp
from jax import lax

D = 768
HEADS = 12
HEAD_DIM = 64
FF = 3072
TFREQ = 128
THID = 512
L = 128
STEP = 10
SEQS = 64
TOKENS = 8192
MATS = 7536640
P_SIZE = 7547136


def layout_scales(index_all):
    extents = [TFREQ * THID, THID * D, 3 * D * D, D * D, D * FF, FF * D, THID, D, D, D, D, D, D, FF, D, D, D]
    spreads = [TFREQ ** (-0.5), THID ** (-0.5), D ** (-0.5), (D // 8) ** (-0.5), D ** (-0.5), FF ** (-0.5), 0.3, 0.3, 0.3, 0.3, 0.3, 0.1, 0.3, 0.3, 0.3, 0.1, 0.3]
    centers = [0.0] * 11 + [1.0, 0.0, 0.0, 0.0, 1.0, 0.0]
    seg_scale = jnp.zeros(index_all.shape, jnp.float32)
    seg_center = jnp.zeros(index_all.shape, jnp.float32)
    offset = 0
    for extent, spread, center in zip(extents, spreads, centers):
        inside = (index_all >= offset) & (index_all < offset + extent)
        seg_scale = jnp.where(inside, spread, seg_scale)
        seg_center = jnp.where(inside, center, seg_center)
        offset += extent
    return (seg_scale, seg_center)


def draw_lengths(key, part):
    key = jax.random.fold_in(key, 1)
    key_long, key_short = jax.random.split(key)
    longish = jax.random.randint(key_long, (SEQS,), 0, 2)
    longish = longish.at[0].set(1)
    short_len = jax.random.randint(key_short, (SEQS,), max(1, L // 4), L // 2 + 1)
    return jnp.where(longish == 1, L, short_len).astype(jnp.int32)


def draw_params(key, part):
    key = jax.random.fold_in(key, 2)
    index_all = jnp.arange(P_SIZE, dtype=jnp.int32)
    seg_scale, seg_center = layout_scales(index_all)
    noise_draw = jnp.clip(jax.random.normal(key, (P_SIZE,), jnp.float32), -4.0, 4.0)
    return noise_draw * seg_scale + seg_center


def draw_moment_one(key, part):
    key = jax.random.fold_in(key, 3)
    grad_size = math.sqrt(TOKENS)
    noise_draw = jnp.clip(jax.random.normal(key, (P_SIZE,), jnp.float32), -4.0, 4.0)
    return noise_draw * grad_size


def draw_moment_two(key, part):
    key = jax.random.fold_in(key, 4)
    grad_size = math.sqrt(TOKENS)
    factor = jnp.exp(jax.random.uniform(key, (P_SIZE,), jnp.float32, 0.0, math.log(4.0)))
    return factor * (grad_size * grad_size)


def set_ends(values, stream_key, least, top_value):
    index_at = [jax.random.randint(jax.random.fold_in(stream_key, axis), (), 0, length) for axis, length in enumerate(values.shape)]
    widest = values.shape.index(max(values.shape))
    beside = index_at[:widest] + [(index_at[widest] + 1) % values.shape[widest]] + index_at[widest + 1:]
    return values.at[tuple(index_at)].set(least).at[tuple(beside)].set(top_value)


def shard_levels(rng, dims, cuts, least, high):
    factor_of, own = 1.0, jax.random.fold_in(rng, 6)
    for position, blocks in cuts:
        steps = jnp.exp(jax.random.uniform(jax.random.fold_in(own, position), (blocks,), jnp.float32, least / len(cuts), high / len(cuts)))
        factor_of = factor_of * jnp.repeat(steps, dims[position] // blocks).reshape([-1 if axis == position else 1 for axis in range(len(dims))])
    return factor_of


def bell_draw(key, dims, scale, limit, cuts=(), kind=jnp.bfloat16):
    array = jax.random.normal(key, dims, jnp.float32) * scale
    if len(cuts) > 0:
        array = shard_levels(key, dims, cuts, -0.22, 0.18) * array
    return jnp.clip(array, min=-limit, max=limit).astype(kind)


def setup_inputs(seed: int = 0) -> dict:
    key_list = jax.random.split(jax.random.key(seed), 8)
    return {
        "tokens": bell_draw(key_list[0], (SEQS, L, D), 1.0, 6.0, ((0, 32),)),
        "lengths": draw_lengths(jax.random.fold_in(key_list[7], 71), 0),
        "timesteps": set_ends(jax.random.randint(key_list[2], (SEQS,), 0, 2000), jax.random.fold_in(key_list[2], 1), 0, 1999).astype(jnp.int32),
        "cotangent": bell_draw(key_list[3], (SEQS, L, D), 1.0, 6.0, ((0, 32),)),
        "params": draw_params(jax.random.fold_in(key_list[7], 71), 0),
        "moment_one": draw_moment_one(jax.random.fold_in(key_list[7], 71), 0),
        "moment_two": draw_moment_two(jax.random.fold_in(key_list[7], 71), 0),
    }


@jax.custom_vjp
def low(v):
    return lax.optimization_barrier(v.astype(jnp.bfloat16)).astype(jnp.float32)

@jax.custom_vjp
def low_back(v):
    return v

def low_keep(v):
    return (low(v), None)

def low_pass(kept, grad):
    return (grad,)

def back_keep(v):
    return (v, None)

def back_low(kept, grad):
    return (low(grad),)
low.defvjp(low_keep, low_pass)
low_back.defvjp(back_keep, back_low)
NORM_EPS = 1e-05
ADAM_EPS = 1e-08
BETA_ONE = 0.5
BETA_TWO = 0.5
RATE_MATRIX = 0.02
RATE_SMALL = 0.2
WEIGHT_DECAY = 0.01

def segment_shapes():
    return [(TFREQ, THID), (THID, D), (D, 3 * D), (D, D), (D, FF), (FF, D), (THID,), (D,), (D,), (D,), (D,), (D,), (D,), (FF,), (D,), (D,), (D,)]

def split_flat(flat_vec):
    pieces = []
    offset = 0
    for seg_shape in segment_shapes():
        extent = math.prod(seg_shape)
        pieces.append(flat_vec[offset:offset + extent].reshape(seg_shape))
        offset += extent
    return pieces

def mat_high(left_mat, right_mat):
    return jnp.dot(left_mat, right_mat, precision=lax.Precision.HIGHEST, preferred_element_type=jnp.float32)

def layer_norm(values, gain_vec, shift_vec):
    center = values - lax.optimization_barrier(jnp.mean(values, axis=-1, keepdims=True))
    variance = lax.optimization_barrier(jnp.mean(center * center, axis=-1, keepdims=True))
    return center * lax.rsqrt(variance + NORM_EPS) * gain_vec + shift_vec

def block_forward(weights, tok_block, step_block, len_block):
    time_in, time_out, qkv_weight, out_weight, up_weight, down_weight, time_in_bias, time_out_bias, q_bias, v_bias, out_bias, gain_one, shift_one, up_bias, down_bias, gain_two, shift_two = weights
    seq_count, length, model_width = tok_block.shape
    half_freq = TFREQ // 2
    frequencies = jnp.exp(-math.log(10000.0) * jnp.arange(half_freq, dtype=jnp.float32) / half_freq)
    angles = step_block.astype(jnp.float32)[:, None] * frequencies[None, :]
    sinusoid = jnp.concatenate([jnp.cos(angles), jnp.sin(angles)], axis=1)
    time_pre = low_back(mat_high(low(sinusoid), time_in) + time_in_bias)
    time_emb = low_back(mat_high(low(jax.nn.silu(time_pre)), time_out) + time_out_bias)
    rows_zero = (tok_block + time_emb[:, None, :]).reshape(seq_count * length, model_width)
    qkv_rows = mat_high(low(rows_zero), qkv_weight)
    quad = (seq_count, length, HEADS, HEAD_DIM)
    q_heads = low_back(low(qkv_rows[:, :model_width] + q_bias)).reshape(quad)
    k_heads = low_back(low(qkv_rows[:, model_width:2 * model_width])).reshape(quad)
    v_heads = low_back(low(qkv_rows[:, 2 * model_width:] + v_bias)).reshape(quad)
    scores = jnp.einsum('bqhd,bkhd->bhqk', q_heads, k_heads, precision=lax.Precision.HIGHEST) * HEAD_DIM ** (-0.5)
    scores = low_back(scores)
    key_valid = jnp.arange(length, dtype=jnp.int32)[None, :] < len_block[:, None]
    scores = jnp.where(key_valid[:, None, None, :], scores, -1e+30)
    attn_probs = jax.nn.softmax(scores, axis=-1)
    context = jnp.einsum('bhqk,bkhd->bqhd', low(attn_probs), v_heads, precision=lax.Precision.HIGHEST)
    context = low_back(low(context.reshape(seq_count * length, model_width)))
    attn_out = low_back(mat_high(context, out_weight) + out_bias)
    hidden_one = layer_norm(rows_zero + attn_out, gain_one, shift_one)
    up_pre = low_back(mat_high(low(hidden_one), up_weight) + up_bias)
    down_out = low_back(mat_high(low(jax.nn.gelu(up_pre, approximate=False)), down_weight) + down_bias)
    result = layer_norm(hidden_one + down_out, gain_two, shift_two)
    return result.reshape(seq_count, length, model_width)

def reference(tokens, lengths, timesteps, cotangent, params, moment_one, moment_two):
    block_seqs = math.gcd(SEQS, max(1, 4096 // L))
    blocks = SEQS // block_seqs

    def forward(flat_vec, tok_all):
        weights = split_flat(low(flat_vec))

        def one_block(block_items):
            return block_forward(weights, block_items[0], block_items[1], block_items[2])
        checked = jax.checkpoint(one_block)
        shaped = (tok_all.reshape(blocks, block_seqs, L, D), timesteps.reshape(blocks, block_seqs), lengths.reshape(blocks, block_seqs))
        return lax.map(checked, shaped).reshape(SEQS, L, D)
    outputs, pullback = jax.vjp(forward, params, tokens.astype(jnp.float32))
    grad_flat, token_grad = pullback(cotangent.astype(jnp.float32))
    moment_new = BETA_ONE * moment_one + (1.0 - BETA_ONE) * grad_flat
    second_new = BETA_TWO * moment_two + (1.0 - BETA_TWO) * grad_flat * grad_flat
    corr_one = 1.0 - BETA_ONE ** STEP
    corr_two = 1.0 - BETA_TWO ** STEP
    index_all = jnp.arange(P_SIZE, dtype=jnp.int32)
    is_matrix = index_all < MATS
    rates = jnp.where(is_matrix, RATE_MATRIX, RATE_SMALL)
    decays = jnp.where(is_matrix, WEIGHT_DECAY, 0.0)
    update = moment_new / corr_one / (jnp.sqrt(second_new / corr_two) + ADAM_EPS)
    new_params = params - rates * (update + decays * params)
    return (outputs.astype(jnp.bfloat16), token_grad, new_params, moment_new, second_new)
```

```python
import math

import jax
import jax.numpy as jnp
from jax import lax
from jax.experimental import pallas as pl
from jax.experimental.pallas import tpu as pltpu
from jax.sharding import PartitionSpec as P

D = 768
HEADS = 12
HEAD_DIM = 64
FF = 3072
TFREQ = 128
THID = 512
STEP = 10
MATS = 7536640
L = 128

NORM_EPS = 1e-05
ADAM_EPS = 1e-08
BETA_ONE = 0.5
BETA_TWO = 0.5
RATE_MATRIX = 0.02
RATE_SMALL = 0.2
WEIGHT_DECAY = 0.01

LANES = 128
ROUND = 16

TIME_IN, TIME_OUT, QKV, OUT, UP, DOWN, VEC = range(7)
MATRICES = [(TFREQ, THID), (THID, D), (D, 3 * D), (D, D), (D, FF), (FF, D), (82, LANES)]
VEC_ROWS = 96
V_TIME_IN, V_TIME_OUT, V_Q, V_V, V_OUT, V_GAIN1, V_SHIFT1, V_UP, V_DOWN, V_GAIN2, V_SHIFT2 = (
    0, 4, 10, 16, 22, 28, 34, 40, 64, 70, 76,
)

F32 = jnp.float32
BF16 = jnp.bfloat16


def up_to(value, step):
    return -(-value // step) * step


class Geometry:
    def __init__(self, total, shards):
        self.shards = shards
        self.length = total // shards
        self.offsets = []
        offset = 0
        for rows, cols in MATRICES:
            self.offsets.append(offset)
            offset += rows * cols
        assert offset == total and total % shards == 0
        self.regions = []
        for index in range(shards):
            low, high = index * self.length, (index + 1) * self.length
            base, found = 0, []
            for matrix, (rows, cols) in enumerate(MATRICES):
                start, stop = max(low, self.offsets[matrix]), min(high, self.offsets[matrix] + rows * cols)
                if start >= stop:
                    continue
                first = (start - self.offsets[matrix]) // cols // ROUND * ROUND
                last = up_to(up_to(stop - self.offsets[matrix], cols) // cols, ROUND)
                found.append((matrix, first, last, base))
                base += (last - first) * (cols // LANES)
            self.regions.append(found)
        used = [
            sum((last - first) * (MATRICES[matrix][1] // LANES) for matrix, first, last, _ in found)
            for found in self.regions
        ]
        self.rows = up_to(max(used), 8 * ROUND)
        self.quarter = self.rows // 4
        self.runs = []
        for matrix, (rows, cols) in enumerate(MATRICES):
            groups = []
            for group in range(up_to(rows, ROUND) // ROUND):
                row = group * ROUND
                places = []
                for index, found in enumerate(self.regions):
                    for which, first, last, base in found:
                        if which == matrix and first <= row < last:
                            places.append((index, first, last, base))
                assert places
                groups.append((row, places))
            runs = []
            for row, places in groups:
                if runs and runs[-1][2] == places:
                    runs[-1][1] = row + ROUND
                else:
                    runs.append([row, row + ROUND, places])
            self.runs.append([tuple(run) for run in runs])
        self.margin = ROUND * (FF // LANES)
        self.flat_rows = up_to(up_to(self.length, LANES) // LANES + 1, 8)
        self.buffer_rows = self.margin + self.flat_rows + self.margin + 8

    def table(self):
        out = []
        for index, found in enumerate(self.regions):
            line = [[0, 0, 0] for _ in MATRICES]
            first_row = index * self.length // LANES
            for matrix, first, last, base in found:
                width = MATRICES[matrix][1] // LANES
                start = self.offsets[matrix] // LANES + first * width - first_row + self.margin
                line[matrix] = [start, (last - first) // ROUND, base]
            out.extend(value for item in line for value in item)
        return jnp.array(out, jnp.int32)


def aligned(value, step=ROUND):
    return value if isinstance(value, int) else pl.multiple_of(value, step)


def spread_steps(length):
    steps = 4
    return steps, up_to(-(-length // steps), 8 * 1024)


def region_loop(table, index, body):
    for matrix, (_, cols) in enumerate(MATRICES):
        width = cols // LANES
        at = (index * len(MATRICES) + matrix) * 3
        start, groups, base = table[at], table[at + 1], table[at + 2]

        def group_step(group, carry, width=width, start=start, groups=groups, base=base):
            for column in range(width):
                flat = start + group * (ROUND * width) + column
                place = pl.multiple_of(base + (column * groups + group) * ROUND, ROUND)
                body(flat, width, place)
            return carry

        lax.fori_loop(0, groups, group_step, 0)


def pack_block(geo, params, where):
    steps, chunk = spread_steps(geo.length)
    rows = chunk // LANES

    def kernel(where_ref, table_ref, params_ref, block_ref, quarter_ref, buffer):
        step = pl.program_id(0)
        index = where_ref[0]
        shift = (index * geo.length) % LANES

        @pl.when(step == 0)
        def _():
            buffer[pl.ds(0, geo.margin), :] = jnp.zeros((geo.margin, LANES), F32)
            tail = geo.margin + geo.flat_rows - 8
            rest = buffer.shape[0] - tail
            buffer[pl.ds(tail, rest), :] = jnp.zeros((rest, LANES), F32)

        place = lax.broadcasted_iota(jnp.int32, (64, LANES), 0) * LANES + lax.broadcasted_iota(
            jnp.int32, (64, LANES), 1
        )

        def roll_in(part, carry):
            value = params_ref[pl.ds(pl.multiple_of(part * 8192, 8192), 8192)].reshape(64, LANES)
            before = step * chunk + part * 8192
            value = jnp.where(place + before < geo.length, value, 0.0)
            at = pl.multiple_of(geo.margin + step * rows + part * 64, 8)
            buffer[pl.ds(at, 64), :] = pltpu.roll(value, shift, 1)
            return carry

        lax.fori_loop(0, chunk // 8192, roll_in, 0)

        @pl.when(step == steps - 1)
        def _():
            late = lax.broadcasted_iota(jnp.int32, (ROUND, LANES), 1) >= shift

            def move(flat, width, place):
                here = buffer[pl.ds(flat, ROUND, stride=width), :]
                above = buffer[pl.ds(flat - 1, ROUND, stride=width), :]
                block_ref[pl.ds(place, ROUND), :] = jnp.where(late, here, above).astype(BF16)

            region_loop(table_ref, index, move)
            mine = pl.multiple_of(where_ref[1] * geo.quarter, ROUND)
            quarter_ref[...] = block_ref[pl.ds(mine, geo.quarter), :]

    buffer_rows = geo.margin + max(steps * rows, geo.flat_rows) + geo.margin + 8
    return pl.pallas_call(
        kernel,
        grid=(steps,),
        in_specs=[
            pl.BlockSpec(memory_space=pltpu.SMEM),
            pl.BlockSpec(memory_space=pltpu.SMEM),
            pl.BlockSpec((chunk,), lambda i: (i,)),
        ],
        out_specs=[
            pl.BlockSpec((geo.rows, LANES), lambda i: (0, 0)),
            pl.BlockSpec((geo.quarter, LANES), lambda i: (0, 0)),
        ],
        out_shape=[
            jax.ShapeDtypeStruct((geo.rows, LANES), BF16),
            jax.ShapeDtypeStruct((geo.quarter, LANES), BF16),
        ],
        scratch_shapes=[pltpu.VMEM((buffer_rows, LANES), F32)],
        compiler_params=pltpu.CompilerParams(vmem_limit_bytes=32 * 2**20),
        name="pack_block",
    )(where, geo.table(), params)


def optimizer_step(geo, params, moment_one, moment_two, where, pieces, piece_places):
    steps, chunk = spread_steps(geo.length)
    rows = chunk // LANES
    count = len(pieces)
    corr_one = 1.0 - BETA_ONE**STEP
    corr_two = 1.0 - BETA_TWO**STEP

    def kernel(where_ref, table_ref, *refs):
        piece_refs = refs[:count]
        params_ref, one_ref, two_ref, new_params_ref, new_one_ref, new_two_ref, block, buffer, sems = refs[count:]
        step = pl.program_id(0)
        index = where_ref[0]
        shift = (index * geo.length) % LANES

        @pl.when(step == 0)
        def _():
            places = piece_places(index, where_ref[1])
            copies = [
                pltpu.make_async_copy(ref, block.at[pl.ds(aligned(at), ref.shape[0]), :], sems.at[i])
                for i, (ref, at) in enumerate(zip(piece_refs, places))
            ]
            for copy in copies:
                copy.start()
            for copy in copies:
                copy.wait()

            def move(flat, width, place):
                buffer[pl.ds(flat, ROUND, stride=width), :] = block[pl.ds(place, ROUND), :].astype(F32)

            region_loop(table_ref, index, move)

        late = lax.broadcasted_iota(jnp.int32, (64, LANES), 1) >= shift
        place = lax.broadcasted_iota(jnp.int32, (64, LANES), 0) * LANES + lax.broadcasted_iota(
            jnp.int32, (64, LANES), 1
        )

        def update(part, carry):
            at = geo.margin + step * rows + part * 64
            here = buffer[pl.ds(pl.multiple_of(at, 8), 64), :]
            below = buffer[pl.ds(at + 1, 64), :]
            grad = pltpu.roll(jnp.where(late, here, below), LANES - shift, 1)
            span = pl.ds(pl.multiple_of(part * 8192, 8192), 8192)
            old = params_ref[span].reshape(64, LANES)
            new_one = BETA_ONE * one_ref[span].reshape(64, LANES) + (1.0 - BETA_ONE) * grad
            new_two = BETA_TWO * two_ref[span].reshape(64, LANES) + (1.0 - BETA_TWO) * grad * grad
            is_matrix = place + (index * geo.length + step * chunk + part * 8192) < MATS
            rates = jnp.where(is_matrix, RATE_MATRIX, RATE_SMALL)
            decays = jnp.where(is_matrix, WEIGHT_DECAY, 0.0)
            change = new_one / corr_one / (jnp.sqrt(new_two / corr_two) + ADAM_EPS)
            new_params_ref[span] = (old - rates * (change + decays * old)).reshape(8192)
            new_one_ref[span] = new_one.reshape(8192)
            new_two_ref[span] = new_two.reshape(8192)
            return carry

        lax.fori_loop(0, chunk // 8192, update, 0)

    buffer_rows = geo.margin + max(steps * rows, geo.flat_rows) + geo.margin + 8
    flat_spec = pl.BlockSpec((chunk,), lambda i: (i,))
    flat_shape = jax.ShapeDtypeStruct((geo.length,), F32)
    return pl.pallas_call(
        kernel,
        grid=(steps,),
        in_specs=[pl.BlockSpec(memory_space=pltpu.SMEM)] * 2
        + [pl.BlockSpec(memory_space=pl.ANY)] * count
        + [flat_spec] * 3,
        out_specs=[flat_spec] * 3,
        out_shape=[flat_shape] * 3,
        scratch_shapes=[
            pltpu.VMEM((geo.rows, LANES), BF16),
            pltpu.VMEM((buffer_rows, LANES), F32),
            pltpu.SemaphoreType.DMA((count,)),
        ],
        compiler_params=pltpu.CompilerParams(vmem_limit_bytes=48 * 2**20),
        name="optimizer_step",
    )(where, geo.table(), *pieces, params, moment_one, moment_two)


def nn(left, right):
    return lax.dot_general(left, right, (((1,), (0,)), ((), ())), preferred_element_type=F32)


def nt(left, right):
    return lax.dot_general(left, right, (((1,), (1,)), ((), ())), preferred_element_type=F32)


def norm_parts(values):
    center = values - jnp.mean(values, axis=-1, keepdims=True)
    inverse = lax.rsqrt(jnp.mean(center * center, axis=-1, keepdims=True) + NORM_EPS)
    return center * inverse, inverse


def norm_back(scaled, hat, inverse):
    return inverse * (
        scaled
        - jnp.mean(scaled, axis=-1, keepdims=True)
        - hat * jnp.mean(scaled * hat, axis=-1, keepdims=True)
    )


def model_step(geo, tokens, cotangent, lengths, sinusoid, where, weights, weight_places, outs_of):
    seqs = tokens.shape[0] // L
    rows = tokens.shape[0]
    count = len(weights)
    pairs = HEADS // 2
    grads = geo.shards
    scale = HEAD_DIM ** (-0.5)

    def kernel(where_ref, lengths_ref, tokens_ref, cotangent_ref, sinusoid_ref, *refs):
        weight_refs = refs[:count]
        refs = refs[count:]
        output_ref, token_grad_ref = refs[:2]
        grad_refs = refs[2 : 2 + grads] if outs_of else refs[2:3]
        (
            store, vecs, vec_grads, rows_zero, rows_low, qkv, probs, context, hat_one, hidden, hidden_low, hidden_t,
            act, slope, total, d_hidden, d_qkv, in_sems, out_sems,
        ) = refs[2 + len(grad_refs) :]

        index, replica = where_ref[0], where_ref[1]
        copies = []
        for i, (ref, (block, at)) in enumerate(zip(weight_refs, weight_places(index, replica))):
            target = store if block is None else store.at[block, pl.ds(aligned(at), ref.shape[0]), :]
            copies.append(pltpu.make_async_copy(ref, target, in_sems.at[i]))
        for copy in copies:
            copy.start()
        for copy in copies:
            copy.wait()

        def spans(matrix, low, high):
            for first, last, places in geo.runs[matrix]:
                start, stop = max(first, low), min(last, high)
                if start < stop:
                    yield start, stop, places

        def ref_rows(place, column, start, stop):
            block, first, last, base = place
            at = base + column * (last - first) + start - first
            return store.at[block, pl.ds(aligned(at), stop - start), :]

        def load(matrix, column, low=0, high=None):
            parts = []
            for start, stop, places in spans(matrix, low, high or up_to(MATRICES[matrix][0], ROUND)):
                value = ref_rows(places[0], column, start, stop)[...]
                for place in places[1:]:
                    value = value + ref_rows(place, column, start, stop)[...]
                parts.append(value)
            return parts[0] if len(parts) == 1 else jnp.concatenate(parts, axis=0)

        def load_wide(matrix, column, wide, low=0, high=None):
            return jnp.concatenate([load(matrix, column + i, low, high) for i in range(wide)], axis=1)

        def save(matrix, column, value, low=0):
            for start, stop, places in spans(matrix, low, low + value.shape[0]):
                for place in places:
                    ref_rows(place, column, start, stop)[...] = value[start - low : stop - low, :]

        def save_wide(matrix, column, value, low=0):
            value = value.astype(BF16)
            for i in range(value.shape[1] // LANES):
                save(matrix, column + i, value[:, i * LANES : (i + 1) * LANES], low)

        def vec(row, wide):
            return jnp.concatenate([vecs[pl.ds(row + i, 1), :] for i in range(wide)], axis=1)

        def vec_grad(row, value):
            sums = jnp.sum(value, axis=0, keepdims=True)
            for i in range(sums.shape[1] // LANES):
                vec_grads[pl.ds(row + i, 1), :] = sums[:, i * LANES : (i + 1) * LANES]

        vecs[...] = load(VEC, 0).astype(F32)
        vec_grads[...] = jnp.zeros((VEC_ROWS, LANES), F32)

        sines = sinusoid_ref[...]
        time_pre = nn(sines, load_wide(TIME_IN, 0, 4)) + vec(V_TIME_IN, 4)
        time_gate = 1.0 / (1.0 + jnp.exp(-time_pre))
        time_act = (time_pre * time_gate).astype(BF16)
        time_emb = nn(time_act, load_wide(TIME_OUT, 0, 6)) + vec(V_TIME_OUT, 6)
        for seq in range(seqs):
            span = pl.ds(seq * L, L)
            value = tokens_ref[span, :].astype(F32) + time_emb[seq : seq + 1, :]
            rows_zero[span, :] = value
            rows_low[span, :] = value.astype(BF16)

        for tile in range(9):
            value = nn(rows_low[...], load_wide(QKV, 2 * tile, 2))
            if tile < 3:
                value = value + vec(V_Q + 2 * tile, 2)
            if tile >= 6:
                value = value + vec(V_V + 2 * (tile - 6), 2)
            qkv[:, tile * 256 : (tile + 1) * 256] = value.astype(BF16)

        first_head = lax.broadcasted_iota(jnp.int32, (L, LANES), 1) < HEAD_DIM

        def split_heads(value):
            zero = jnp.zeros_like(value)
            return jnp.concatenate([jnp.where(first_head, value, zero), jnp.where(first_head, zero, value)], axis=0)

        def both(value):
            return jnp.concatenate([jnp.broadcast_to(item, (L, L)) for item in value], axis=1)

        def pair_at(seq, pair, part):
            return qkv[pl.ds(seq * L, L), pl.ds(part * D + pair * LANES, LANES)]

        key = lax.broadcasted_iota(jnp.int32, (L, 2 * L), 1) % L
        for seq in range(seqs):
            valid = key < lengths_ref[seq]
            for pair in range(pairs):
                scores = nt(pair_at(seq, pair, 0), split_heads(pair_at(seq, pair, 1))) * scale
                scores = jnp.where(valid, scores, -1e30)
                top = both([jnp.max(scores[:, i * L : (i + 1) * L], axis=1, keepdims=True) for i in range(2)])
                power = jnp.exp(scores - top)
                sums = [jnp.sum(power[:, i * L : (i + 1) * L], axis=1, keepdims=True) for i in range(2)]
                weight = power * both([1.0 / item for item in sums])
                probs[seq * pairs + pair] = weight
                value = nn(weight.astype(BF16), split_heads(pair_at(seq, pair, 2)))
                context[pl.ds(seq * L, L), pl.ds(pair * LANES, LANES)] = value.astype(BF16)

        for tile in range(3):
            cols = pl.ds(tile * 256, 256)
            value = nn(context[...], load_wide(OUT, 2 * tile, 2)) + vec(V_OUT + 2 * tile, 2)
            total[:, cols] = rows_zero[:, cols] + value
        hat, inverse_one = norm_parts(total[...])
        hat_one[...] = hat
        gain_one = vec(V_GAIN1, 6)
        value = hat * gain_one + vec(V_SHIFT1, 6)
        hidden[...] = value
        hidden_low[...] = value.astype(BF16)
        hidden_t[...] = value.astype(BF16).T

        def up_step(tile, carry):
            pre = nn(hidden_low[...], load_wide(UP, 2 * tile, 2)) + vec(V_UP + 2 * tile, 2)
            below = 0.5 * (1.0 + lax.erf(pre * (0.5**0.5)))
            cols = pl.ds(aligned(tile * 256, 256), 256)
            act[:, cols] = (pre * below).astype(BF16)
            slope[:, cols] = below + pre * (jnp.exp(-0.5 * pre * pre) * (1.0 / math.sqrt(2.0 * math.pi)))
            return carry

        lax.fori_loop(0, 12, up_step, 0)
        for tile in range(3):
            cols = pl.ds(tile * 256, 256)
            value = nn(act[...], load_wide(DOWN, 2 * tile, 2)) + vec(V_DOWN + 2 * tile, 2)
            total[:, cols] = hidden[:, cols] + value

        hat, inverse = norm_parts(total[...])
        gain_two = vec(V_GAIN2, 6)
        output_ref[...] = (hat * gain_two + vec(V_SHIFT2, 6)).astype(BF16)
        d_result = cotangent_ref[...].astype(F32)
        vec_grad(V_GAIN2, d_result * hat)
        vec_grad(V_SHIFT2, d_result)
        value = norm_back(d_result * gain_two, hat, inverse)
        d_hidden[...] = value
        d_down = value.astype(BF16)
        vec_grad(V_DOWN, d_down.astype(F32))

        for tile in range(12):
            low, high = tile * 256, (tile + 1) * 256
            cols = pl.ds(low, 256)
            d_act = nt(d_down, load_wide(DOWN, 0, 6, low, high))
            save_wide(DOWN, 0, nn(act[:, cols].T, d_down), low)
            d_up = (d_act * slope[:, cols]).astype(BF16)
            vec_grad(V_UP + 2 * tile, d_up.astype(F32))
            d_hidden[...] += nt(d_up, load_wide(UP, 2 * tile, 2))
            save_wide(UP, 2 * tile, nn(hidden_t[...], d_up))

        d_out = d_hidden[...]
        hat = hat_one[...]
        vec_grad(V_GAIN1, d_out * hat)
        vec_grad(V_SHIFT1, d_out)
        value = norm_back(d_out * gain_one, hat, inverse_one)
        total[...] = value
        d_attn = value.astype(BF16)
        vec_grad(V_OUT, d_attn.astype(F32))
        d_context = nt(d_attn, load_wide(OUT, 0, 6)).astype(BF16)
        context_t = context[...].T
        for tile in range(3):
            save_wide(OUT, 2 * tile, nn(context_t, d_attn[:, tile * 256 : (tile + 1) * 256]))
        context[...] = d_context

        for seq in range(seqs):
            span = pl.ds(seq * L, L)
            for pair in range(pairs):
                weight = probs[seq * pairs + pair]
                d_pair = context[span, pl.ds(pair * LANES, LANES)]
                query, keys = pair_at(seq, pair, 0), pair_at(seq, pair, 1)
                d_weight = nt(d_pair, split_heads(pair_at(seq, pair, 2)))
                mixed = weight * d_weight
                delta = both([jnp.sum(mixed[:, i * L : (i + 1) * L], axis=1, keepdims=True) for i in range(2)])
                d_scores = (weight * (d_weight - delta)).astype(BF16)
                d_query = nn(d_scores, split_heads(keys)) * scale
                stacked = nn(d_scores.T, query)
                d_key = jnp.where(first_head, stacked[:L], stacked[L:]) * scale
                stacked = nn(weight.astype(BF16).T, d_pair)
                d_value = jnp.where(first_head, stacked[:L], stacked[L:])
                for part, item in enumerate((d_query, d_key, d_value)):
                    d_qkv[span, pl.ds(part * D + pair * LANES, LANES)] = item.astype(BF16)

        rows_t = rows_low[...].T
        for tile in range(9):
            value = d_qkv[:, tile * 256 : (tile + 1) * 256]
            if tile < 3:
                vec_grad(V_Q + 2 * tile, value.astype(F32))
            if tile >= 6:
                vec_grad(V_V + 2 * (tile - 6), value.astype(F32))
            total[...] += nt(value, load_wide(QKV, 2 * tile, 2))
            save_wide(QKV, 2 * tile, nn(rows_t, value))
        d_rows = total[...]
        token_grad_ref[...] = d_rows

        d_time = [jnp.sum(d_rows[seq * L : (seq + 1) * L], axis=0, keepdims=True) for seq in range(seqs)]
        d_time = jnp.concatenate(d_time + [jnp.zeros((sines.shape[0] - seqs, D), F32)], axis=0).astype(BF16)
        vec_grad(V_TIME_OUT, d_time.astype(F32))
        d_time_act = nt(d_time, load_wide(TIME_OUT, 0, 6))
        save_wide(TIME_OUT, 0, nn(time_act.T, d_time))
        d_time_pre = (d_time_act * (time_gate * (1.0 + time_pre * (1.0 - time_gate)))).astype(BF16)
        vec_grad(V_TIME_IN, d_time_pre.astype(F32))
        save_wide(TIME_IN, 0, nn(sines.T, d_time_pre))
        save(VEC, 0, vec_grads[...].astype(BF16))

        if outs_of:
            copies = [
                pltpu.make_async_copy(store.at[block], ref, out_sems.at[i])
                for i, (ref, block) in enumerate(zip(grad_refs, outs_of(index)))
            ]
        else:
            copies = [pltpu.make_async_copy(store, grad_refs[0], out_sems.at[0])]
        for copy in copies:
            copy.start()
        for copy in copies:
            copy.wait()

    if outs_of:
        grad_shapes = [jax.ShapeDtypeStruct((geo.rows, LANES), BF16)] * grads
    else:
        grad_shapes = [jax.ShapeDtypeStruct((geo.shards, geo.rows, LANES), BF16)]
    whole = pl.BlockSpec(memory_space=pltpu.VMEM)
    return pl.pallas_call(
        kernel,
        in_specs=[pl.BlockSpec(memory_space=pltpu.SMEM)] * 2
        + [whole] * 3
        + [pl.BlockSpec(memory_space=pl.ANY)] * count,
        out_specs=[whole] * 2 + [pl.BlockSpec(memory_space=pl.ANY)] * len(grad_shapes),
        out_shape=[jax.ShapeDtypeStruct((rows, D), BF16), jax.ShapeDtypeStruct((rows, D), F32)] + grad_shapes,
        scratch_shapes=[
            pltpu.VMEM((geo.shards, geo.rows, LANES), BF16),
            pltpu.VMEM((VEC_ROWS, LANES), F32),
            pltpu.VMEM((VEC_ROWS, LANES), F32),
            pltpu.VMEM((rows, D), F32),
            pltpu.VMEM((rows, D), BF16),
            pltpu.VMEM((rows, 3 * D), BF16),
            pltpu.VMEM((seqs * pairs, L, 2 * L), F32),
            pltpu.VMEM((rows, D), BF16),
            pltpu.VMEM((rows, D), F32),
            pltpu.VMEM((rows, D), F32),
            pltpu.VMEM((rows, D), BF16),
            pltpu.VMEM((D, rows), BF16),
            pltpu.VMEM((rows, FF), BF16),
            pltpu.VMEM((rows, FF), F32),
            pltpu.VMEM((rows, D), F32),
            pltpu.VMEM((rows, D), F32),
            pltpu.VMEM((rows, 3 * D), BF16),
            pltpu.SemaphoreType.DMA((count,)),
            pltpu.SemaphoreType.DMA((len(grad_shapes),)),
        ],
        compiler_params=pltpu.CompilerParams(vmem_limit_bytes=60 * 2**20),
        name="model_step",
    )(where, lengths, tokens, cotangent, sinusoid, *weights)


def neighbor_quarters(index, replica):
    core = index % 2
    return replica, replica ^ (1 + core), replica ^ (2 - core), replica ^ 3


def add_cores(geo, keep, got, where):
    size = geo.quarter

    def kernel(where_ref, keep_ref, got_ref, near_ref, far_ref):
        order = neighbor_quarters(where_ref[0], where_ref[1])
        for i, quarter in enumerate(order):
            span = pl.ds(pl.multiple_of(quarter * size, ROUND), size)
            value = (keep_ref[span, :].astype(F32) + got_ref[span, :].astype(F32)).astype(BF16)
            (near_ref if i < 2 else far_ref)[i % 2] = value

    whole = pl.BlockSpec(memory_space=pltpu.VMEM)
    return pl.pallas_call(
        kernel,
        in_specs=[pl.BlockSpec(memory_space=pltpu.SMEM), whole, whole],
        out_specs=[whole, whole],
        out_shape=[jax.ShapeDtypeStruct((2, size, LANES), BF16)] * 2,
        compiler_params=pltpu.CompilerParams(vmem_limit_bytes=32 * 2**20),
        name="add_cores",
    )(where, keep, got)


def add_pair(near, got):
    size = near.shape[1]

    def kernel(near_ref, got_ref, own_ref, next_ref):
        for i, ref in enumerate((own_ref, next_ref)):
            ref[...] = (near_ref[i].astype(F32) + got_ref[i].astype(F32)).astype(BF16)

    whole = pl.BlockSpec(memory_space=pltpu.VMEM)
    return pl.pallas_call(
        kernel,
        in_specs=[whole, whole],
        out_specs=[whole, whole],
        out_shape=[jax.ShapeDtypeStruct((size, LANES), BF16)] * 2,
        compiler_params=pltpu.CompilerParams(vmem_limit_bytes=32 * 2**20),
        name="add_pair",
    )(near, got)


def add_all(*items):
    def kernel(*refs):
        value = refs[0][...].astype(F32)
        for ref in refs[1:-1]:
            value = value + ref[...].astype(F32)
        refs[-1][...] = value.astype(BF16)

    whole = pl.BlockSpec(memory_space=pltpu.VMEM)
    return pl.pallas_call(
        kernel,
        in_specs=[whole] * len(items),
        out_specs=whole,
        out_shape=jax.ShapeDtypeStruct(items[0].shape, BF16),
        compiler_params=pltpu.CompilerParams(vmem_limit_bytes=32 * 2**20),
        name="add_all",
    )(*items)


def ring_order(size):
    return list(range(0, size, 2))[:1] + list(range(1, size, 2)) + list(range(size - 2, 0, -2))


def select(value, choices):
    out = jnp.int32(choices[0])
    for i, choice in enumerate(choices[1:], 1):
        out = jnp.where(value == i, choice, out)
    return out


def make_local(dp, fsdp):
    direct = dp == 4 and fsdp == 8
    chips = fsdp // 2
    order = ring_order(chips)
    before = [order[order.index(chip) - 1] for chip in range(chips)]

    def chip_before(chip, hops):
        table = list(range(chips))
        for _ in range(hops):
            table = [before[item] for item in table]
        return select(chip, table)

    def permute(value, axes, target):
        pairs = []
        for replica in range(dp):
            for index in range(fsdp):
                pairs.append((replica * fsdp + index, target(replica, index)))
        return lax.ppermute(value, axes, pairs)

    def core_swap(value):
        return lax.ppermute(value, "fsdp", [(index, index ^ 1) for index in range(fsdp)])

    def ring_hop(value):
        return lax.ppermute(
            value, "fsdp", [(before[chip] * 2 + core, chip * 2 + core) for chip in range(chips) for core in range(2)]
        )

    def first_way(value):
        return permute(value, ("dp", "fsdp"), lambda r, i: (r ^ (1 + i % 2)) * fsdp + i)

    def second_way(value):
        return permute(value, ("dp", "fsdp"), lambda r, i: (r ^ (2 - i % 2)) * fsdp + i)

    def local(tokens, lengths, timesteps, cotangent, params, moment_one, moment_two):
        geo = Geometry(params.shape[0] * fsdp, fsdp)
        where = jnp.stack([lax.axis_index("fsdp"), lax.axis_index("dp")]).astype(jnp.int32)
        seqs = tokens.shape[0]

        half_freq = TFREQ // 2
        frequencies = jnp.exp(-math.log(10000.0) * jnp.arange(half_freq, dtype=F32) / half_freq)
        angles = timesteps.astype(F32)[:, None] * frequencies[None, :]
        sinusoid = jnp.concatenate([jnp.cos(angles), jnp.sin(angles)], axis=1).astype(BF16)
        sinusoid = jnp.pad(sinusoid, ((0, up_to(seqs, ROUND) - seqs), (0, 0)))

        block, quarter = pack_block(geo, params, where)

        if direct:
            weights = [block, core_swap(block)]
            for _ in range(1, chips):
                quarter = ring_hop(quarter)
                one = first_way(quarter)
                two = second_way(quarter)
                three = second_way(one)
                four = [quarter, one, two, three]
                weights += four + [core_swap(item) for item in four]

            def weight_places(index, replica):
                chip, core = index // 2, index % 2
                places = [(index, 0), (index ^ 1, 0)]
                for hops in range(1, chips):
                    for whose in (index, index ^ 1):
                        source = chip_before(chip, hops) * 2 + whose % 2
                        places += [(source, item * geo.quarter) for item in neighbor_quarters(whose, replica)]
                return places

            def outs_of(index):
                chip, core = index // 2, index % 2
                out = []
                for hops in range(1, chips + 1):
                    other = chip_before(chip, hops)
                    out += [other * 2 + core, other * 2 + 1 - core]
                return out

        else:
            weights = [lax.all_gather(block, "fsdp", axis=0)]

            def weight_places(index, replica):
                return [(None, 0)]

            outs_of = None

        output, token_grad, *grads = model_step(
            geo,
            tokens.reshape(seqs * L, D),
            cotangent.reshape(seqs * L, D),
            lengths,
            sinusoid,
            where,
            weights,
            weight_places,
            outs_of,
        )

        if direct:
            passed = []
            for hops in range(chips):
                keep, send = grads[2 * hops], grads[2 * hops + 1]
                near, far = add_cores(geo, keep, core_swap(send), where)
                own, other = add_pair(near, second_way(far))
                quarter = add_all(own, first_way(other), *passed)
                if hops < chips - 1:
                    passed = [ring_hop(quarter)]
            one = first_way(quarter)
            pieces = [quarter, one, second_way(quarter), second_way(one)]

            def piece_places(index, replica):
                return [item * geo.quarter for item in neighbor_quarters(index, replica)]

        else:
            mine = lax.psum_scatter(grads[0], "fsdp", scatter_dimension=0)
            pieces = [lax.psum(mine, "dp")]

            def piece_places(index, replica):
                return [0]

        new_params, new_one, new_two = optimizer_step(
            geo, params, moment_one, moment_two, where, pieces, piece_places
        )
        return (
            output.reshape(tokens.shape),
            token_grad.reshape(tokens.shape),
            new_params,
            new_one,
            new_two,
        )

    return local


def solution(mesh):
    batch = P(("dp", "fsdp"))
    rows = P(("dp", "fsdp"), None, None)
    flat = P("fsdp")
    return jax.shard_map(
        make_local(mesh.shape["dp"], mesh.shape["fsdp"]),
        mesh=mesh,
        in_specs=(rows, batch, batch, rows, flat, flat, flat),
        out_specs=(rows, rows, flat, flat, flat),
        check_vma=False,
    )
```

```python
import math

import jax
import jax.numpy as jnp
from jax import lax
from jax.experimental import pallas as pl
from jax.experimental.pallas import tpu as pltpu
from jax.sharding import PartitionSpec as P

D = 768
HEADS = 12
HEAD_DIM = 64
FF = 3072
TFREQ = 128
THID = 512
STEP = 10
MATS = 7536640
L = 128

NORM_EPS = 1e-05
ADAM_EPS = 1e-08
BETA_ONE = 0.5
BETA_TWO = 0.5
RATE_MATRIX = 0.02
RATE_SMALL = 0.2
WEIGHT_DECAY = 0.01

LANES = 128
ROUND = 16

TIME_IN, TIME_OUT, QKV, OUT, UP, DOWN, VEC = range(7)
MATRICES = [(TFREQ, THID), (THID, D), (D, 3 * D), (D, D), (D, FF), (FF, D), (82, LANES)]
VEC_ROWS = 96
V_TIME_IN, V_TIME_OUT, V_Q, V_V, V_OUT, V_GAIN1, V_SHIFT1, V_UP, V_DOWN, V_GAIN2, V_SHIFT2 = (
    0, 4, 10, 16, 22, 28, 34, 40, 64, 70, 76,
)

F32 = jnp.float32
BF16 = jnp.bfloat16


def up_to(value, step):
    return -(-value // step) * step


class Geometry:
    def __init__(self, total, shards):
        self.shards = shards
        self.length = total // shards
        self.offsets = []
        offset = 0
        for rows, cols in MATRICES:
            self.offsets.append(offset)
            offset += rows * cols
        assert offset == total and total % shards == 0
        self.regions = []
        for index in range(shards):
            low, high = index * self.length, (index + 1) * self.length
            base, found = 0, []
            for matrix, (rows, cols) in enumerate(MATRICES):
                start, stop = max(low, self.offsets[matrix]), min(high, self.offsets[matrix] + rows * cols)
                if start >= stop:
                    continue
                first = (start - self.offsets[matrix]) // cols // ROUND * ROUND
                last = up_to(up_to(stop - self.offsets[matrix], cols) // cols, ROUND)
                found.append((matrix, first, last, base))
                base += (last - first) * (cols // LANES)
            self.regions.append(found)
        used = [
            sum((last - first) * (MATRICES[matrix][1] // LANES) for matrix, first, last, _ in found)
            for found in self.regions
        ]
        self.rows = up_to(max(used), 8 * ROUND)
        self.quarter = self.rows // 4
        self.runs = []
        for matrix, (rows, cols) in enumerate(MATRICES):
            groups = []
            for group in range(up_to(rows, ROUND) // ROUND):
                row = group * ROUND
                places = []
                for index, found in enumerate(self.regions):
                    for which, first, last, base in found:
                        if which == matrix and first <= row < last:
                            places.append((index, first, last, base))
                assert places
                groups.append((row, places))
            runs = []
            for row, places in groups:
                if runs and runs[-1][2] == places:
                    runs[-1][1] = row + ROUND
                else:
                    runs.append([row, row + ROUND, places])
            self.runs.append([tuple(run) for run in runs])
        self.attention_blocks = max(i for i, found in enumerate(self.regions) if found[0][0] < UP)
        self.vector_blocks = min(i for i, found in enumerate(self.regions) if found[-1][0] == VEC)
        self.margin = ROUND * (FF // LANES)
        self.flat_rows = up_to(up_to(self.length, LANES) // LANES + 1, 8)
        self.buffer_rows = self.margin + self.flat_rows + self.margin + 8

    def table(self):
        out = []
        for index, found in enumerate(self.regions):
            line = [[0, 0, 0] for _ in MATRICES]
            first_row = index * self.length // LANES
            for matrix, first, last, base in found:
                width = MATRICES[matrix][1] // LANES
                start = self.offsets[matrix] // LANES + first * width - first_row + self.margin
                line[matrix] = [start, (last - first) // ROUND, base]
            out.extend(value for item in line for value in item)
        return jnp.array(out, jnp.int32)


def aligned(value, step=ROUND):
    return value if isinstance(value, int) else pl.multiple_of(value, step)


def spread_steps(length):
    steps = 4
    return steps, up_to(-(-length // steps), 8 * 1024)


def region_loop(table, index, body):
    for matrix, (_, cols) in enumerate(MATRICES):
        width = cols // LANES
        at = (index * len(MATRICES) + matrix) * 3
        start, groups, base = table[at], table[at + 1], table[at + 2]

        def group_step(group, carry, width=width, start=start, groups=groups, base=base):
            for column in range(width):
                flat = start + group * (ROUND * width) + column
                place = pl.multiple_of(base + (column * groups + group) * ROUND, ROUND)
                body(flat, width, place)
            return carry

        lax.fori_loop(0, groups, group_step, 0)


def pack_block(geo, params, where):
    steps, chunk = spread_steps(geo.length)
    rows = chunk // LANES

    def kernel(where_ref, table_ref, params_ref, block_ref, quarter_ref, buffer):
        step = pl.program_id(0)
        index = where_ref[0]
        shift = (index * geo.length) % LANES

        @pl.when(step == 0)
        def _():
            buffer[pl.ds(0, geo.margin), :] = jnp.zeros((geo.margin, LANES), F32)
            tail = geo.margin + geo.flat_rows - 8
            rest = buffer.shape[0] - tail
            buffer[pl.ds(tail, rest), :] = jnp.zeros((rest, LANES), F32)

        place = lax.broadcasted_iota(jnp.int32, (64, LANES), 0) * LANES + lax.broadcasted_iota(
            jnp.int32, (64, LANES), 1
        )

        def roll_in(part, carry):
            value = params_ref[pl.ds(pl.multiple_of(part * 8192, 8192), 8192)].reshape(64, LANES)
            before = step * chunk + part * 8192
            value = jnp.where(place + before < geo.length, value, 0.0)
            at = pl.multiple_of(geo.margin + step * rows + part * 64, 8)
            buffer[pl.ds(at, 64), :] = pltpu.roll(value, shift, 1)
            return carry

        lax.fori_loop(0, chunk // 8192, roll_in, 0, unroll=True)

        @pl.when(step == steps - 1)
        def _():
            late = lax.broadcasted_iota(jnp.int32, (ROUND, LANES), 1) >= shift

            def move(flat, width, place):
                here = buffer[pl.ds(flat, ROUND, stride=width), :]
                above = buffer[pl.ds(flat - 1, ROUND, stride=width), :]
                block_ref[pl.ds(place, ROUND), :] = jnp.where(late, here, above).astype(BF16)

            region_loop(table_ref, index, move)
            mine = pl.multiple_of(where_ref[1] * geo.quarter, ROUND)
            quarter_ref[...] = block_ref[pl.ds(mine, geo.quarter), :]

    buffer_rows = geo.margin + max(steps * rows, geo.flat_rows) + geo.margin + 8
    return pl.pallas_call(
        kernel,
        grid=(steps,),
        in_specs=[
            pl.BlockSpec(memory_space=pltpu.SMEM),
            pl.BlockSpec(memory_space=pltpu.SMEM),
            pl.BlockSpec((chunk,), lambda i: (i,)),
        ],
        out_specs=[
            pl.BlockSpec((geo.rows, LANES), lambda i: (0, 0)),
            pl.BlockSpec((geo.quarter, LANES), lambda i: (0, 0)),
        ],
        out_shape=[
            jax.ShapeDtypeStruct((geo.rows, LANES), BF16),
            jax.ShapeDtypeStruct((geo.quarter, LANES), BF16),
        ],
        scratch_shapes=[pltpu.VMEM((buffer_rows, LANES), F32)],
        compiler_params=pltpu.CompilerParams(vmem_limit_bytes=32 * 2**20),
        name="pack_block",
    )(where, geo.table(), params)


def optimizer_step(geo, params, moment_one, moment_two, where, pieces, piece_places):
    steps, chunk = spread_steps(geo.length)
    rows = chunk // LANES
    count = len(pieces)
    corr_one = 1.0 - BETA_ONE**STEP
    corr_two = 1.0 - BETA_TWO**STEP

    def kernel(where_ref, table_ref, *refs):
        piece_refs = refs[:count]
        params_ref, one_ref, two_ref, new_params_ref, new_one_ref, new_two_ref, block, buffer, sems = refs[count:]
        step = pl.program_id(0)
        index = where_ref[0]
        shift = (index * geo.length) % LANES

        @pl.when(step == 0)
        def _():
            places = piece_places(index, where_ref[1])
            copies = [
                pltpu.make_async_copy(ref, block.at[pl.ds(aligned(at), ref.shape[0]), :], sems.at[i])
                for i, (ref, at) in enumerate(zip(piece_refs, places))
            ]
            for copy in copies:
                copy.start()
            for copy in copies:
                copy.wait()

            def move(flat, width, place):
                buffer[pl.ds(flat, ROUND, stride=width), :] = block[pl.ds(place, ROUND), :].astype(F32)

            region_loop(table_ref, index, move)

        late = lax.broadcasted_iota(jnp.int32, (64, LANES), 1) >= shift
        place = lax.broadcasted_iota(jnp.int32, (64, LANES), 0) * LANES + lax.broadcasted_iota(
            jnp.int32, (64, LANES), 1
        )

        def update(part, carry):
            at = geo.margin + step * rows + part * 64
            here = buffer[pl.ds(pl.multiple_of(at, 8), 64), :]
            below = buffer[pl.ds(at + 1, 64), :]
            grad = pltpu.roll(jnp.where(late, here, below), LANES - shift, 1)
            span = pl.ds(pl.multiple_of(part * 8192, 8192), 8192)
            old = params_ref[span].reshape(64, LANES)
            new_one = BETA_ONE * one_ref[span].reshape(64, LANES) + (1.0 - BETA_ONE) * grad
            new_two = BETA_TWO * two_ref[span].reshape(64, LANES) + (1.0 - BETA_TWO) * grad * grad
            is_matrix = place + (index * geo.length + step * chunk + part * 8192) < MATS
            rates = jnp.where(is_matrix, RATE_MATRIX, RATE_SMALL)
            decays = jnp.where(is_matrix, WEIGHT_DECAY, 0.0)
            change = new_one / corr_one / (jnp.sqrt(new_two / corr_two) + ADAM_EPS)
            new_params_ref[span] = (old - rates * (change + decays * old)).reshape(8192)
            new_one_ref[span] = new_one.reshape(8192)
            new_two_ref[span] = new_two.reshape(8192)
            return carry

        lax.fori_loop(0, chunk // 8192, update, 0, unroll=True)

    buffer_rows = geo.margin + max(steps * rows, geo.flat_rows) + geo.margin + 8
    flat_spec = pl.BlockSpec((chunk,), lambda i: (i,))
    flat_shape = jax.ShapeDtypeStruct((geo.length,), F32)
    return pl.pallas_call(
        kernel,
        grid=(steps,),
        in_specs=[pl.BlockSpec(memory_space=pltpu.SMEM)] * 2
        + [pl.BlockSpec(memory_space=pl.ANY)] * count
        + [flat_spec] * 3,
        out_specs=[flat_spec] * 3,
        out_shape=[flat_shape] * 3,
        scratch_shapes=[
            pltpu.VMEM((geo.rows, LANES), BF16),
            pltpu.VMEM((buffer_rows, LANES), F32),
            pltpu.SemaphoreType.DMA((count,)),
        ],
        compiler_params=pltpu.CompilerParams(vmem_limit_bytes=48 * 2**20),
        name="optimizer_step",
    )(where, geo.table(), *pieces, params, moment_one, moment_two)


def nn(left, right):
    return lax.dot_general(left, right, (((1,), (0,)), ((), ())), preferred_element_type=F32)


def nt(left, right):
    return lax.dot_general(left, right, (((1,), (1,)), ((), ())), preferred_element_type=F32)


def norm_parts(values):
    center = values - jnp.mean(values, axis=-1, keepdims=True)
    inverse = lax.rsqrt(jnp.mean(center * center, axis=-1, keepdims=True) + NORM_EPS)
    return center * inverse, inverse


def norm_back(scaled, hat, inverse):
    return inverse * (
        scaled
        - jnp.mean(scaled, axis=-1, keepdims=True)
        - hat * jnp.mean(scaled * hat, axis=-1, keepdims=True)
    )


def model_step(geo, tokens, cotangent, lengths, sinusoid, where, weights, weight_places, outs_of):
    seqs = tokens.shape[0] // L
    rows = tokens.shape[0]
    count = len(weights)
    pairs = HEADS // 2
    grads = geo.shards
    scale = HEAD_DIM ** (-0.5)

    def kernel(where_ref, lengths_ref, tokens_ref, cotangent_ref, sinusoid_ref, *refs):
        weight_refs = refs[:count]
        refs = refs[count:]
        output_ref, token_grad_ref = refs[:2]
        grad_refs = refs[2 : 2 + grads] if outs_of else refs[2:3]
        (
            store, vecs, vec_grads, rows_zero, rows_low, qkv, probs, context, hat_one, hidden, hidden_low, hidden_t,
            act, slope, total, d_hidden, d_qkv, in_sems, out_sems,
        ) = refs[2 + len(grad_refs) :]

        index, replica = where_ref[0], where_ref[1]
        arrivals = []
        for i, (ref, (block, at)) in enumerate(zip(weight_refs, weight_places(index, replica))):
            target = store if block is None else store.at[block, pl.ds(aligned(at), ref.shape[0]), :]
            arrivals.append((block, pltpu.make_async_copy(ref, target, in_sems.at[i])))

        def each_arrival(early, act):
            for block, copy in arrivals:
                if block is None:
                    if early:
                        act(copy)
                else:
                    first = (block <= geo.attention_blocks) | (block >= geo.vector_blocks)
                    pl.when(first if early else jnp.logical_not(first))(lambda copy=copy: act(copy))

        each_arrival(True, lambda copy: copy.start())
        each_arrival(False, lambda copy: copy.start())
        each_arrival(True, lambda copy: copy.wait())

        def spans(matrix, low, high):
            for first, last, places in geo.runs[matrix]:
                start, stop = max(first, low), min(last, high)
                if start < stop:
                    yield start, stop, places

        def ref_rows(place, column, start, stop):
            block, first, last, base = place
            at = base + column * (last - first) + start - first
            return store.at[block, pl.ds(aligned(at), stop - start), :]

        def load(matrix, column, low=0, high=None):
            parts = []
            for start, stop, places in spans(matrix, low, high or up_to(MATRICES[matrix][0], ROUND)):
                value = ref_rows(places[0], column, start, stop)[...]
                for place in places[1:]:
                    value = value + ref_rows(place, column, start, stop)[...]
                parts.append(value)
            return parts[0] if len(parts) == 1 else jnp.concatenate(parts, axis=0)

        def load_wide(matrix, column, wide, low=0, high=None):
            return jnp.concatenate([load(matrix, column + i, low, high) for i in range(wide)], axis=1)

        def save(matrix, column, value, low=0):
            for start, stop, places in spans(matrix, low, low + value.shape[0]):
                for place in places:
                    ref_rows(place, column, start, stop)[...] = value[start - low : stop - low, :]

        def save_wide(matrix, column, value, low=0):
            value = value.astype(BF16)
            for i in range(value.shape[1] // LANES):
                save(matrix, column + i, value[:, i * LANES : (i + 1) * LANES], low)

        def vec(row, wide):
            return jnp.concatenate([vecs[pl.ds(row + i, 1), :] for i in range(wide)], axis=1)

        def vec_grad(row, value):
            sums = jnp.sum(value, axis=0, keepdims=True)
            for i in range(sums.shape[1] // LANES):
                vec_grads[pl.ds(row + i, 1), :] = sums[:, i * LANES : (i + 1) * LANES]

        vecs[...] = load(VEC, 0).astype(F32)
        vec_grads[...] = jnp.zeros((VEC_ROWS, LANES), F32)

        sines = sinusoid_ref[...]
        time_pre = nn(sines, load_wide(TIME_IN, 0, 4)) + vec(V_TIME_IN, 4)
        time_gate = 1.0 / (1.0 + jnp.exp(-time_pre))
        time_act = (time_pre * time_gate).astype(BF16)
        time_emb = nn(time_act, load_wide(TIME_OUT, 0, 6)) + vec(V_TIME_OUT, 6)
        for seq in range(seqs):
            span = pl.ds(seq * L, L)
            value = tokens_ref[span, :].astype(F32) + time_emb[seq : seq + 1, :]
            rows_zero[span, :] = value
            rows_low[span, :] = value.astype(BF16)

        for tile in range(9):
            value = nn(rows_low[...], load_wide(QKV, 2 * tile, 2))
            if tile < 3:
                value = value + vec(V_Q + 2 * tile, 2)
            if tile >= 6:
                value = value + vec(V_V + 2 * (tile - 6), 2)
            qkv[:, tile * 256 : (tile + 1) * 256] = value.astype(BF16)

        first_head = lax.broadcasted_iota(jnp.int32, (L, LANES), 1) < HEAD_DIM

        def split_heads(value):
            zero = jnp.zeros_like(value)
            return jnp.concatenate([jnp.where(first_head, value, zero), jnp.where(first_head, zero, value)], axis=0)

        def both(value):
            return jnp.concatenate([jnp.broadcast_to(item, (L, L)) for item in value], axis=1)

        def pair_at(seq, pair, part):
            return qkv[pl.ds(seq * L, L), pl.ds(part * D + pair * LANES, LANES)]

        key = lax.broadcasted_iota(jnp.int32, (L, 2 * L), 1) % L
        for seq in range(seqs):
            valid = key < lengths_ref[seq]
            for pair in range(pairs):
                scores = nt(pair_at(seq, pair, 0), split_heads(pair_at(seq, pair, 1))) * scale
                scores = jnp.where(valid, scores, -1e30)
                top = both([jnp.max(scores[:, i * L : (i + 1) * L], axis=1, keepdims=True) for i in range(2)])
                power = jnp.exp(scores - top)
                sums = [jnp.sum(power[:, i * L : (i + 1) * L], axis=1, keepdims=True) for i in range(2)]
                weight = power * both([1.0 / item for item in sums])
                probs[seq * pairs + pair] = weight
                value = nn(weight.astype(BF16), split_heads(pair_at(seq, pair, 2)))
                context[pl.ds(seq * L, L), pl.ds(pair * LANES, LANES)] = value.astype(BF16)

        for tile in range(3):
            cols = pl.ds(tile * 256, 256)
            value = nn(context[...], load_wide(OUT, 2 * tile, 2)) + vec(V_OUT + 2 * tile, 2)
            total[:, cols] = rows_zero[:, cols] + value
        hat, inverse_one = norm_parts(total[...])
        hat_one[...] = hat
        gain_one = vec(V_GAIN1, 6)
        value = hat * gain_one + vec(V_SHIFT1, 6)
        hidden[...] = value
        hidden_low[...] = value.astype(BF16)
        hidden_t[...] = value.astype(BF16).T

        each_arrival(False, lambda copy: copy.wait())

        def up_step(tile, carry):
            pre = nn(hidden_low[...], load_wide(UP, 2 * tile, 2)) + vec(V_UP + 2 * tile, 2)
            below = 0.5 * (1.0 + lax.erf(pre * (0.5**0.5)))
            cols = pl.ds(aligned(tile * 256, 256), 256)
            act[:, cols] = (pre * below).astype(BF16)
            slope[:, cols] = below + pre * (jnp.exp(-0.5 * pre * pre) * (1.0 / math.sqrt(2.0 * math.pi)))
            return carry

        lax.fori_loop(0, 12, up_step, 0)
        for tile in range(3):
            cols = pl.ds(tile * 256, 256)
            value = nn(act[...], load_wide(DOWN, 2 * tile, 2)) + vec(V_DOWN + 2 * tile, 2)
            total[:, cols] = hidden[:, cols] + value

        hat, inverse = norm_parts(total[...])
        gain_two = vec(V_GAIN2, 6)
        output_ref[...] = (hat * gain_two + vec(V_SHIFT2, 6)).astype(BF16)
        d_result = cotangent_ref[...].astype(F32)
        vec_grad(V_GAIN2, d_result * hat)
        vec_grad(V_SHIFT2, d_result)
        value = norm_back(d_result * gain_two, hat, inverse)
        d_hidden[...] = value
        d_down = value.astype(BF16)
        vec_grad(V_DOWN, d_down.astype(F32))

        for tile in range(12):
            low, high = tile * 256, (tile + 1) * 256
            cols = pl.ds(low, 256)
            d_act = nt(d_down, load_wide(DOWN, 0, 6, low, high))
            save_wide(DOWN, 0, nn(act[:, cols].T, d_down), low)
            d_up = (d_act * slope[:, cols]).astype(BF16)
            vec_grad(V_UP + 2 * tile, d_up.astype(F32))
            d_hidden[...] += nt(d_up, load_wide(UP, 2 * tile, 2))
            save_wide(UP, 2 * tile, nn(hidden_t[...], d_up))

        if outs_of:
            departures = [
                (block, pltpu.make_async_copy(store.at[block], ref, out_sems.at[i]))
                for i, (ref, block) in enumerate(zip(grad_refs, outs_of(index)))
            ]
        else:
            departures = [(None, pltpu.make_async_copy(store, grad_refs[0], out_sems.at[0]))]

        def each_departure(early, act):
            for block, copy in departures:
                if block is None:
                    if not early:
                        act(copy)
                else:
                    first = (block > geo.attention_blocks) & (block < geo.vector_blocks)
                    pl.when(first if early else jnp.logical_not(first))(lambda copy=copy: act(copy))

        each_departure(True, lambda copy: copy.start())

        d_out = d_hidden[...]
        hat = hat_one[...]
        vec_grad(V_GAIN1, d_out * hat)
        vec_grad(V_SHIFT1, d_out)
        value = norm_back(d_out * gain_one, hat, inverse_one)
        total[...] = value
        d_attn = value.astype(BF16)
        vec_grad(V_OUT, d_attn.astype(F32))
        d_context = nt(d_attn, load_wide(OUT, 0, 6)).astype(BF16)
        context_t = context[...].T
        for tile in range(3):
            save_wide(OUT, 2 * tile, nn(context_t, d_attn[:, tile * 256 : (tile + 1) * 256]))
        context[...] = d_context

        for seq in range(seqs):
            span = pl.ds(seq * L, L)
            for pair in range(pairs):
                weight = probs[seq * pairs + pair]
                d_pair = context[span, pl.ds(pair * LANES, LANES)]
                query, keys = pair_at(seq, pair, 0), pair_at(seq, pair, 1)
                d_weight = nt(d_pair, split_heads(pair_at(seq, pair, 2)))
                mixed = weight * d_weight
                delta = both([jnp.sum(mixed[:, i * L : (i + 1) * L], axis=1, keepdims=True) for i in range(2)])
                d_scores = (weight * (d_weight - delta)).astype(BF16)
                d_query = nn(d_scores, split_heads(keys)) * scale
                stacked = nn(d_scores.T, query)
                d_key = jnp.where(first_head, stacked[:L], stacked[L:]) * scale
                stacked = nn(weight.astype(BF16).T, d_pair)
                d_value = jnp.where(first_head, stacked[:L], stacked[L:])
                for part, item in enumerate((d_query, d_key, d_value)):
                    d_qkv[span, pl.ds(part * D + pair * LANES, LANES)] = item.astype(BF16)

        rows_t = rows_low[...].T
        for tile in range(9):
            value = d_qkv[:, tile * 256 : (tile + 1) * 256]
            if tile < 3:
                vec_grad(V_Q + 2 * tile, value.astype(F32))
            if tile >= 6:
                vec_grad(V_V + 2 * (tile - 6), value.astype(F32))
            total[...] += nt(value, load_wide(QKV, 2 * tile, 2))
            save_wide(QKV, 2 * tile, nn(rows_t, value))
        d_rows = total[...]
        token_grad_ref[...] = d_rows

        d_time = [jnp.sum(d_rows[seq * L : (seq + 1) * L], axis=0, keepdims=True) for seq in range(seqs)]
        d_time = jnp.concatenate(d_time + [jnp.zeros((sines.shape[0] - seqs, D), F32)], axis=0).astype(BF16)
        vec_grad(V_TIME_OUT, d_time.astype(F32))
        d_time_act = nt(d_time, load_wide(TIME_OUT, 0, 6))
        save_wide(TIME_OUT, 0, nn(time_act.T, d_time))
        d_time_pre = (d_time_act * (time_gate * (1.0 + time_pre * (1.0 - time_gate)))).astype(BF16)
        vec_grad(V_TIME_IN, d_time_pre.astype(F32))
        save_wide(TIME_IN, 0, nn(sines.T, d_time_pre))
        save(VEC, 0, vec_grads[...].astype(BF16))

        each_departure(False, lambda copy: copy.start())
        each_departure(True, lambda copy: copy.wait())
        each_departure(False, lambda copy: copy.wait())

    if outs_of:
        grad_shapes = [jax.ShapeDtypeStruct((geo.rows, LANES), BF16)] * grads
    else:
        grad_shapes = [jax.ShapeDtypeStruct((geo.shards, geo.rows, LANES), BF16)]
    whole = pl.BlockSpec(memory_space=pltpu.VMEM)
    return pl.pallas_call(
        kernel,
        in_specs=[pl.BlockSpec(memory_space=pltpu.SMEM)] * 2
        + [whole] * 3
        + [pl.BlockSpec(memory_space=pl.ANY)] * count,
        out_specs=[whole] * 2 + [pl.BlockSpec(memory_space=pl.ANY)] * len(grad_shapes),
        out_shape=[jax.ShapeDtypeStruct((rows, D), BF16), jax.ShapeDtypeStruct((rows, D), F32)] + grad_shapes,
        scratch_shapes=[
            pltpu.VMEM((geo.shards, geo.rows, LANES), BF16),
            pltpu.VMEM((VEC_ROWS, LANES), F32),
            pltpu.VMEM((VEC_ROWS, LANES), F32),
            pltpu.VMEM((rows, D), F32),
            pltpu.VMEM((rows, D), BF16),
            pltpu.VMEM((rows, 3 * D), BF16),
            pltpu.VMEM((seqs * pairs, L, 2 * L), F32),
            pltpu.VMEM((rows, D), BF16),
            pltpu.VMEM((rows, D), F32),
            pltpu.VMEM((rows, D), F32),
            pltpu.VMEM((rows, D), BF16),
            pltpu.VMEM((D, rows), BF16),
            pltpu.VMEM((rows, FF), BF16),
            pltpu.VMEM((rows, FF), F32),
            pltpu.VMEM((rows, D), F32),
            pltpu.VMEM((rows, D), F32),
            pltpu.VMEM((rows, 3 * D), BF16),
            pltpu.SemaphoreType.DMA((count,)),
            pltpu.SemaphoreType.DMA((len(grad_shapes),)),
        ],
        compiler_params=pltpu.CompilerParams(vmem_limit_bytes=60 * 2**20),
        name="model_step",
    )(where, lengths, tokens, cotangent, sinusoid, *weights)


def neighbor_quarters(index, replica):
    core = index % 2
    return replica, replica ^ (1 + core), replica ^ (2 - core), replica ^ 3


def add_cores(geo, keep, got, where):
    size = geo.quarter

    def kernel(where_ref, keep_ref, got_ref, near_ref, far_ref):
        order = neighbor_quarters(where_ref[0], where_ref[1])
        for i, quarter in enumerate(order):
            span = pl.ds(pl.multiple_of(quarter * size, ROUND), size)
            value = (keep_ref[span, :].astype(F32) + got_ref[span, :].astype(F32)).astype(BF16)
            (near_ref if i < 2 else far_ref)[i % 2] = value

    whole = pl.BlockSpec(memory_space=pltpu.VMEM)
    return pl.pallas_call(
        kernel,
        in_specs=[pl.BlockSpec(memory_space=pltpu.SMEM), whole, whole],
        out_specs=[whole, whole],
        out_shape=[jax.ShapeDtypeStruct((2, size, LANES), BF16)] * 2,
        compiler_params=pltpu.CompilerParams(vmem_limit_bytes=32 * 2**20),
        name="add_cores",
    )(where, keep, got)


def add_pair(near, got):
    size = near.shape[1]

    def kernel(near_ref, got_ref, own_ref, next_ref):
        for i, ref in enumerate((own_ref, next_ref)):
            ref[...] = (near_ref[i].astype(F32) + got_ref[i].astype(F32)).astype(BF16)

    whole = pl.BlockSpec(memory_space=pltpu.VMEM)
    return pl.pallas_call(
        kernel,
        in_specs=[whole, whole],
        out_specs=[whole, whole],
        out_shape=[jax.ShapeDtypeStruct((size, LANES), BF16)] * 2,
        compiler_params=pltpu.CompilerParams(vmem_limit_bytes=32 * 2**20),
        name="add_pair",
    )(near, got)


def add_all(*items):
    def kernel(*refs):
        value = refs[0][...].astype(F32)
        for ref in refs[1:-1]:
            value = value + ref[...].astype(F32)
        refs[-1][...] = value.astype(BF16)

    whole = pl.BlockSpec(memory_space=pltpu.VMEM)
    return pl.pallas_call(
        kernel,
        in_specs=[whole] * len(items),
        out_specs=whole,
        out_shape=jax.ShapeDtypeStruct(items[0].shape, BF16),
        compiler_params=pltpu.CompilerParams(vmem_limit_bytes=32 * 2**20),
        name="add_all",
    )(*items)


def ring_order(size):
    return list(range(0, size, 2))[:1] + list(range(1, size, 2)) + list(range(size - 2, 0, -2))


def select(value, choices):
    out = jnp.int32(choices[0])
    for i, choice in enumerate(choices[1:], 1):
        out = jnp.where(value == i, choice, out)
    return out


def make_local(dp, fsdp):
    direct = dp == 4 and fsdp == 8
    chips = fsdp // 2
    order = ring_order(chips)
    before = [order[order.index(chip) - 1] for chip in range(chips)]

    def chip_before(chip, hops):
        table = list(range(chips))
        for _ in range(hops):
            table = [before[item] for item in table]
        return select(chip, table)

    def permute(value, axes, target):
        pairs = []
        for replica in range(dp):
            for index in range(fsdp):
                pairs.append((replica * fsdp + index, target(replica, index)))
        return lax.ppermute(value, axes, pairs)

    def core_swap(value):
        return lax.ppermute(value, "fsdp", [(index, index ^ 1) for index in range(fsdp)])

    def ring_hop(value):
        return lax.ppermute(
            value, "fsdp", [(before[chip] * 2 + core, chip * 2 + core) for chip in range(chips) for core in range(2)]
        )

    def first_way(value):
        return permute(value, ("dp", "fsdp"), lambda r, i: (r ^ (1 + i % 2)) * fsdp + i)

    def second_way(value):
        return permute(value, ("dp", "fsdp"), lambda r, i: (r ^ (2 - i % 2)) * fsdp + i)

    def local(tokens, lengths, timesteps, cotangent, params, moment_one, moment_two):
        geo = Geometry(params.shape[0] * fsdp, fsdp)
        where = jnp.stack([lax.axis_index("fsdp"), lax.axis_index("dp")]).astype(jnp.int32)
        seqs = tokens.shape[0]

        half_freq = TFREQ // 2
        frequencies = jnp.exp(-math.log(10000.0) * jnp.arange(half_freq, dtype=F32) / half_freq)
        angles = timesteps.astype(F32)[:, None] * frequencies[None, :]
        sinusoid = jnp.concatenate([jnp.cos(angles), jnp.sin(angles)], axis=1).astype(BF16)
        sinusoid = jnp.pad(sinusoid, ((0, up_to(seqs, ROUND) - seqs), (0, 0)))

        block, quarter = pack_block(geo, params, where)

        if direct:
            weights = [block, core_swap(block)]
            one = None
            for _ in range(1, chips):
                quarter = ring_hop(quarter)
                ready = quarter
                if one is not None:
                    ready, one = lax.optimization_barrier((quarter, one))
                one = first_way(ready)
                two = second_way(ready)
                three = second_way(one)
                four = [quarter, one, two, three]
                weights += four + [core_swap(item) for item in four]

            def weight_places(index, replica):
                chip, core = index // 2, index % 2
                places = [(index, 0), (index ^ 1, 0)]
                for hops in range(1, chips):
                    for whose in (index, index ^ 1):
                        source = chip_before(chip, hops) * 2 + whose % 2
                        places += [(source, item * geo.quarter) for item in neighbor_quarters(whose, replica)]
                return places

            def outs_of(index):
                chip, core = index // 2, index % 2
                out = []
                for hops in range(1, chips + 1):
                    other = chip_before(chip, hops)
                    out += [other * 2 + core, other * 2 + 1 - core]
                return out

        else:
            weights = [lax.all_gather(block, "fsdp", axis=0)]

            def weight_places(index, replica):
                return [(None, 0)]

            outs_of = None

        output, token_grad, *grads = model_step(
            geo,
            tokens.reshape(seqs * L, D),
            cotangent.reshape(seqs * L, D),
            lengths,
            sinusoid,
            where,
            weights,
            weight_places,
            outs_of,
        )

        if direct:
            passed = []
            for hops in range(chips):
                keep, send = grads[2 * hops], grads[2 * hops + 1]
                near, far = add_cores(geo, keep, core_swap(send), where)
                own, other = add_pair(near, second_way(far))
                quarter = add_all(own, first_way(other), *passed)
                if hops < chips - 1:
                    passed = [ring_hop(quarter)]
            one = first_way(quarter)
            pieces = [quarter, one, second_way(quarter), second_way(one)]

            def piece_places(index, replica):
                return [item * geo.quarter for item in neighbor_quarters(index, replica)]

        else:
            mine = lax.psum_scatter(grads[0], "fsdp", scatter_dimension=0)
            pieces = [lax.psum(mine, "dp")]

            def piece_places(index, replica):
                return [0]

        new_params, new_one, new_two = optimizer_step(
            geo, params, moment_one, moment_two, where, pieces, piece_places
        )
        return (
            output.reshape(tokens.shape),
            token_grad.reshape(tokens.shape),
            new_params,
            new_one,
            new_two,
        )

    return local


def solution(mesh):
    batch = P(("dp", "fsdp"))
    rows = P(("dp", "fsdp"), None, None)
    flat = P("fsdp")
    return jax.shard_map(
        make_local(mesh.shape["dp"], mesh.shape["fsdp"]),
        mesh=mesh,
        in_specs=(rows, batch, batch, rows, flat, flat, flat),
        out_specs=(rows, rows, flat, flat, flat),
        check_vma=False,
    )
```

```python
import math

import jax
import jax.numpy as jnp
from jax import lax
from jax.experimental import pallas as pl
from jax.experimental.pallas import tpu as pltpu
from jax.sharding import PartitionSpec as P

D = 768
HEADS = 12
HEAD_DIM = 64
FF = 3072
TFREQ = 128
THID = 512
STEP = 10
MATS = 7536640
L = 128

NORM_EPS = 1e-05
ADAM_EPS = 1e-08
BETA_ONE = 0.5
BETA_TWO = 0.5
RATE_MATRIX = 0.02
RATE_SMALL = 0.2
WEIGHT_DECAY = 0.01

LANES = 128
ROUND = 16

TIME_IN, TIME_OUT, QKV, OUT, UP, DOWN, VEC = range(7)
MATRICES = [(TFREQ, THID), (THID, D), (D, 3 * D), (D, D), (D, FF), (FF, D), (82, LANES)]
VEC_ROWS = 96
V_TIME_IN, V_TIME_OUT, V_Q, V_V, V_OUT, V_GAIN1, V_SHIFT1, V_UP, V_DOWN, V_GAIN2, V_SHIFT2 = (
    0, 4, 10, 16, 22, 28, 34, 40, 64, 70, 76,
)

F32 = jnp.float32
BF16 = jnp.bfloat16
TOKEN = (8, LANES)
HEAD = 0.50


def up_to(value, step):
    return -(-value // step) * step


class Geometry:
    def __init__(self, total, shards):
        self.shards = shards
        self.length = total // shards
        self.offsets = []
        offset = 0
        for rows, cols in MATRICES:
            self.offsets.append(offset)
            offset += rows * cols
        assert offset == total and total % shards == 0
        self.regions = []
        for index in range(shards):
            low, high = index * self.length, (index + 1) * self.length
            base, found = 0, []
            for matrix, (rows, cols) in enumerate(MATRICES):
                start, stop = max(low, self.offsets[matrix]), min(high, self.offsets[matrix] + rows * cols)
                if start >= stop:
                    continue
                first = (start - self.offsets[matrix]) // cols // ROUND * ROUND
                last = up_to(up_to(stop - self.offsets[matrix], cols) // cols, ROUND)
                found.append((matrix, first, last, base))
                base += (last - first) * (cols // LANES)
            self.regions.append(found)
        used = [
            sum((last - first) * (MATRICES[matrix][1] // LANES) for matrix, first, last, _ in found)
            for found in self.regions
        ]
        self.rows = up_to(max(used), 8 * ROUND)
        self.quarter = self.rows // 4
        self.head = up_to(int(self.quarter * HEAD), ROUND)
        self.runs = []
        for matrix, (rows, cols) in enumerate(MATRICES):
            groups = []
            for group in range(up_to(rows, ROUND) // ROUND):
                row = group * ROUND
                places = []
                for index, found in enumerate(self.regions):
                    for which, first, last, base in found:
                        if which == matrix and first <= row < last:
                            places.append((index, first, last, base))
                assert places
                groups.append((row, places))
            runs = []
            for row, places in groups:
                if runs and runs[-1][2] == places:
                    runs[-1][1] = row + ROUND
                else:
                    runs.append([row, row + ROUND, places])
            self.runs.append([tuple(run) for run in runs])
        self.attention_blocks = max(i for i, found in enumerate(self.regions) if found[0][0] < UP)
        self.vector_blocks = min(i for i, found in enumerate(self.regions) if found[-1][0] == VEC)
        self.margin = ROUND * (FF // LANES)
        self.flat_rows = up_to(up_to(self.length, LANES) // LANES + 1, 8)
        self.buffer_rows = self.margin + self.flat_rows + self.margin + 8

    def table(self):
        out = []
        for index, found in enumerate(self.regions):
            line = [[0, 0, 0] for _ in MATRICES]
            first_row = index * self.length // LANES
            for matrix, first, last, base in found:
                width = MATRICES[matrix][1] // LANES
                start = self.offsets[matrix] // LANES + first * width - first_row + self.margin
                line[matrix] = [start, (last - first) // ROUND, base]
            out.extend(value for item in line for value in item)
        return jnp.array(out, jnp.int32)


def aligned(value, step=ROUND):
    return value if isinstance(value, int) else pl.multiple_of(value, step)


def spread_steps(length):
    steps = 4
    return steps, up_to(-(-length // steps), 8 * 1024)


def region_loop(table, index, body):
    for matrix, (_, cols) in enumerate(MATRICES):
        width = cols // LANES
        at = (index * len(MATRICES) + matrix) * 3
        start, groups, base = table[at], table[at + 1], table[at + 2]

        def group_step(group, carry, width=width, start=start, groups=groups, base=base):
            for column in range(width):
                flat = start + group * (ROUND * width) + column
                place = pl.multiple_of(base + (column * groups + group) * ROUND, ROUND)
                body(flat, width, place)
            return carry

        lax.fori_loop(0, groups, group_step, 0)


def pack_block(geo, params, where):
    steps, chunk = spread_steps(geo.length)
    rows = chunk // LANES

    def kernel(where_ref, table_ref, params_ref, block_ref, quarter_ref, buffer):
        step = pl.program_id(0)
        index = where_ref[0]
        shift = (index * geo.length) % LANES

        @pl.when(step == 0)
        def _():
            buffer[pl.ds(0, geo.margin), :] = jnp.zeros((geo.margin, LANES), F32)
            tail = geo.margin + geo.flat_rows - 8
            rest = buffer.shape[0] - tail
            buffer[pl.ds(tail, rest), :] = jnp.zeros((rest, LANES), F32)

        place = lax.broadcasted_iota(jnp.int32, (64, LANES), 0) * LANES + lax.broadcasted_iota(
            jnp.int32, (64, LANES), 1
        )

        def roll_in(part, carry):
            value = params_ref[pl.ds(pl.multiple_of(part * 8192, 8192), 8192)].reshape(64, LANES)
            before = step * chunk + part * 8192
            value = jnp.where(place + before < geo.length, value, 0.0)
            at = pl.multiple_of(geo.margin + step * rows + part * 64, 8)
            buffer[pl.ds(at, 64), :] = pltpu.roll(value, shift, 1)
            return carry

        lax.fori_loop(0, chunk // 8192, roll_in, 0, unroll=True)

        @pl.when(step == steps - 1)
        def _():
            late = lax.broadcasted_iota(jnp.int32, (ROUND, LANES), 1) >= shift

            def move(flat, width, place):
                here = buffer[pl.ds(flat, ROUND, stride=width), :]
                above = buffer[pl.ds(flat - 1, ROUND, stride=width), :]
                block_ref[pl.ds(place, ROUND), :] = jnp.where(late, here, above).astype(BF16)

            region_loop(table_ref, index, move)
            mine = pl.multiple_of(where_ref[1] * geo.quarter, ROUND)
            quarter_ref[...] = block_ref[pl.ds(mine, geo.quarter), :]

    buffer_rows = geo.margin + max(steps * rows, geo.flat_rows) + geo.margin + 8
    sizes = [geo.rows, geo.quarter]
    return pl.pallas_call(
        kernel,
        grid=(steps,),
        in_specs=[
            pl.BlockSpec(memory_space=pltpu.SMEM),
            pl.BlockSpec(memory_space=pltpu.SMEM),
            pl.BlockSpec((chunk,), lambda i: (i,)),
        ],
        out_specs=[pl.BlockSpec(memory_space=pltpu.VMEM)] * len(sizes),
        out_shape=[jax.ShapeDtypeStruct((size, LANES), BF16) for size in sizes],
        scratch_shapes=[pltpu.VMEM((buffer_rows, LANES), F32)],
        compiler_params=pltpu.CompilerParams(vmem_limit_bytes=16 * 2**20),
        name="pack_block",
    )(where, geo.table(), params)


def optimizer_step(geo, params, moment_one, moment_two, where, pieces, piece_places):
    steps, chunk = spread_steps(geo.length)
    rows = chunk // LANES
    count = len(pieces)
    corr_one = 1.0 - BETA_ONE**STEP
    corr_two = 1.0 - BETA_TWO**STEP

    def kernel(where_ref, table_ref, *refs):
        piece_refs = refs[:count]
        params_ref, one_ref, two_ref, new_params_ref, new_one_ref, new_two_ref, block, buffer = refs[count:]
        step = pl.program_id(0)
        index = where_ref[0]
        shift = (index * geo.length) % LANES

        @pl.when(step == 0)
        def _():
            for piece, start, length, at in piece_places(index, where_ref[1]):
                block[pl.ds(aligned(at), length), :] = piece_refs[piece][pl.ds(start, length), :]

            def move(flat, width, place):
                buffer[pl.ds(flat, ROUND, stride=width), :] = block[pl.ds(place, ROUND), :].astype(F32)

            region_loop(table_ref, index, move)

        late = lax.broadcasted_iota(jnp.int32, (64, LANES), 1) >= shift
        place = lax.broadcasted_iota(jnp.int32, (64, LANES), 0) * LANES + lax.broadcasted_iota(
            jnp.int32, (64, LANES), 1
        )

        def update(part, carry):
            at = geo.margin + step * rows + part * 64
            here = buffer[pl.ds(pl.multiple_of(at, 8), 64), :]
            below = buffer[pl.ds(at + 1, 64), :]
            grad = pltpu.roll(jnp.where(late, here, below), LANES - shift, 1)
            span = pl.ds(pl.multiple_of(part * 8192, 8192), 8192)
            old = params_ref[span].reshape(64, LANES)
            new_one = BETA_ONE * one_ref[span].reshape(64, LANES) + (1.0 - BETA_ONE) * grad
            new_two = BETA_TWO * two_ref[span].reshape(64, LANES) + (1.0 - BETA_TWO) * grad * grad
            is_matrix = place + (index * geo.length + step * chunk + part * 8192) < MATS
            rates = jnp.where(is_matrix, RATE_MATRIX, RATE_SMALL)
            decays = jnp.where(is_matrix, WEIGHT_DECAY, 0.0)
            change = new_one / corr_one / (jnp.sqrt(new_two / corr_two) + ADAM_EPS)
            new_params_ref[span] = (old - rates * (change + decays * old)).reshape(8192)
            new_one_ref[span] = new_one.reshape(8192)
            new_two_ref[span] = new_two.reshape(8192)
            return carry

        lax.fori_loop(0, chunk // 8192, update, 0, unroll=True)

    buffer_rows = geo.margin + max(steps * rows, geo.flat_rows) + geo.margin + 8
    flat_spec = pl.BlockSpec((chunk,), lambda i: (i,))
    flat_shape = jax.ShapeDtypeStruct((geo.length,), F32)
    return pl.pallas_call(
        kernel,
        grid=(steps,),
        in_specs=[pl.BlockSpec(memory_space=pltpu.SMEM)] * 2
        + [pl.BlockSpec(memory_space=pltpu.VMEM)] * count
        + [flat_spec] * 3,
        out_specs=[flat_spec] * 3,
        out_shape=[flat_shape] * 3,
        scratch_shapes=[
            pltpu.VMEM((geo.rows, LANES), BF16),
            pltpu.VMEM((buffer_rows, LANES), F32),
        ],
        compiler_params=pltpu.CompilerParams(vmem_limit_bytes=24 * 2**20),
        name="optimizer_step",
    )(where, geo.table(), *pieces, params, moment_one, moment_two)


def nn(left, right):
    return lax.dot_general(left, right, (((1,), (0,)), ((), ())), preferred_element_type=F32)


def nt(left, right):
    return lax.dot_general(left, right, (((1,), (1,)), ((), ())), preferred_element_type=F32)


def norm_parts(values):
    center = values - jnp.mean(values, axis=-1, keepdims=True)
    inverse = lax.rsqrt(jnp.mean(center * center, axis=-1, keepdims=True) + NORM_EPS)
    return center * inverse, inverse


def norm_back(scaled, hat, inverse):
    return inverse * (
        scaled
        - jnp.mean(scaled, axis=-1, keepdims=True)
        - hat * jnp.mean(scaled * hat, axis=-1, keepdims=True)
    )


def model_step(geo, tokens, cotangent, lengths, sinusoid, where, pieces, piece_places, grad_parts):
    seqs = tokens.shape[0] // L
    rows = tokens.shape[0]
    count = len(pieces)
    pairs = HEADS // 2
    scale = HEAD_DIM ** (-0.5)
    grad_shapes = [
        ((geo.shards if blocks is None else len(blocks), length, LANES)) for blocks, _, length in grad_parts(0)
    ]
    in_count = sum(geo.shards if isinstance(runs, int) else len(runs) for runs in piece_places(0, 0))
    out_count = sum(shape[0] for shape in grad_shapes)

    def kernel(where_ref, lengths_ref, tokens_ref, cotangent_ref, sinusoid_ref, *refs):
        piece_refs = refs[:count]
        refs = refs[count:]
        output_ref, token_grad_ref = refs[:2]
        grad_refs = refs[2 : 2 + len(grad_shapes)]
        (
            store, vecs, vec_grads, rows_zero, rows_low, qkv, probs, context, hat_one, hidden, hidden_low, hidden_t,
            act, slope, total, d_hidden, d_qkv, in_sems, out_sems,
        ) = refs[2 + len(grad_shapes) :]

        index, replica = where_ref[0], where_ref[1]

        def in_waves(copies, is_early, early, act):
            for block, copy in copies:
                now = is_early(block)
                if isinstance(block, int):
                    if early == now:
                        act(copy)
                else:
                    pl.when(now if early else jnp.logical_not(now))(lambda copy=copy: act(copy))

        arrivals = []
        for ref, runs in zip(piece_refs, piece_places(index, replica)):
            if isinstance(runs, int):
                runs = [(block, None, ref.shape[1], runs) for block in range(geo.shards)]
            for block, start, length, at in runs:
                source = ref.at[block] if start is None else ref.at[pl.ds(start, length), :]
                target = store.at[block, pl.ds(aligned(at), length), :]
                arrivals.append((block, pltpu.make_async_copy(source, target, in_sems.at[len(arrivals)])))

        def read_first(block):
            early, late = block <= geo.attention_blocks, block >= geo.vector_blocks
            return early or late if isinstance(block, int) else early | late

        in_waves(arrivals, read_first, True, lambda copy: copy.start())
        in_waves(arrivals, read_first, False, lambda copy: copy.start())
        in_waves(arrivals, read_first, True, lambda copy: copy.wait())

        def spans(matrix, low, high):
            for first, last, places in geo.runs[matrix]:
                start, stop = max(first, low), min(last, high)
                if start < stop:
                    yield start, stop, places

        def ref_rows(place, column, start, stop):
            block, first, last, base = place
            at = base + column * (last - first) + start - first
            return store.at[block, pl.ds(aligned(at), stop - start), :]

        def load(matrix, column, low=0, high=None):
            parts = []
            for start, stop, places in spans(matrix, low, high or up_to(MATRICES[matrix][0], ROUND)):
                value = ref_rows(places[0], column, start, stop)[...]
                for place in places[1:]:
                    value = value + ref_rows(place, column, start, stop)[...]
                parts.append(value)
            return parts[0] if len(parts) == 1 else jnp.concatenate(parts, axis=0)

        def load_wide(matrix, column, wide, low=0, high=None):
            return jnp.concatenate([load(matrix, column + i, low, high) for i in range(wide)], axis=1)

        def save(matrix, column, value, low=0):
            for start, stop, places in spans(matrix, low, low + value.shape[0]):
                for place in places:
                    ref_rows(place, column, start, stop)[...] = value[start - low : stop - low, :]

        def save_wide(matrix, column, value, low=0):
            value = value.astype(BF16)
            for i in range(value.shape[1] // LANES):
                save(matrix, column + i, value[:, i * LANES : (i + 1) * LANES], low)

        def vec(row, wide):
            return jnp.concatenate([vecs[pl.ds(row + i, 1), :] for i in range(wide)], axis=1)

        def vec_grad(row, value):
            sums = jnp.sum(value, axis=0, keepdims=True)
            for i in range(sums.shape[1] // LANES):
                vec_grads[pl.ds(row + i, 1), :] = sums[:, i * LANES : (i + 1) * LANES]

        vecs[...] = load(VEC, 0).astype(F32)
        vec_grads[...] = jnp.zeros((VEC_ROWS, LANES), F32)

        sines = sinusoid_ref[...]
        time_pre = nn(sines, load_wide(TIME_IN, 0, 4)) + vec(V_TIME_IN, 4)
        time_gate = 1.0 / (1.0 + jnp.exp(-time_pre))
        time_act = (time_pre * time_gate).astype(BF16)
        time_emb = nn(time_act, load_wide(TIME_OUT, 0, 6)) + vec(V_TIME_OUT, 6)
        for seq in range(seqs):
            span = pl.ds(seq * L, L)
            value = tokens_ref[span, :].astype(F32) + time_emb[seq : seq + 1, :]
            rows_zero[span, :] = value
            rows_low[span, :] = value.astype(BF16)

        for tile in range(9):
            value = nn(rows_low[...], load_wide(QKV, 2 * tile, 2))
            if tile < 3:
                value = value + vec(V_Q + 2 * tile, 2)
            if tile >= 6:
                value = value + vec(V_V + 2 * (tile - 6), 2)
            qkv[:, tile * 256 : (tile + 1) * 256] = value.astype(BF16)

        first_head = lax.broadcasted_iota(jnp.int32, (L, LANES), 1) < HEAD_DIM

        def split_heads(value):
            zero = jnp.zeros_like(value)
            return jnp.concatenate([jnp.where(first_head, value, zero), jnp.where(first_head, zero, value)], axis=0)

        def both(value):
            return jnp.concatenate([jnp.broadcast_to(item, (L, L)) for item in value], axis=1)

        def pair_at(seq, pair, part):
            return qkv[pl.ds(seq * L, L), pl.ds(part * D + pair * LANES, LANES)]

        key = lax.broadcasted_iota(jnp.int32, (L, 2 * L), 1) % L
        for seq in range(seqs):
            valid = key < lengths_ref[seq]
            for pair in range(pairs):
                scores = nt(pair_at(seq, pair, 0), split_heads(pair_at(seq, pair, 1))) * scale
                scores = jnp.where(valid, scores, -1e30)
                top = both([jnp.max(scores[:, i * L : (i + 1) * L], axis=1, keepdims=True) for i in range(2)])
                power = jnp.exp(scores - top)
                sums = [jnp.sum(power[:, i * L : (i + 1) * L], axis=1, keepdims=True) for i in range(2)]
                weight = power * both([1.0 / item for item in sums])
                probs[seq * pairs + pair] = weight
                value = nn(weight.astype(BF16), split_heads(pair_at(seq, pair, 2)))
                context[pl.ds(seq * L, L), pl.ds(pair * LANES, LANES)] = value.astype(BF16)

        for tile in range(3):
            cols = pl.ds(tile * 256, 256)
            value = nn(context[...], load_wide(OUT, 2 * tile, 2)) + vec(V_OUT + 2 * tile, 2)
            total[:, cols] = rows_zero[:, cols] + value
        hat, inverse_one = norm_parts(total[...])
        hat_one[...] = hat
        gain_one = vec(V_GAIN1, 6)
        value = hat * gain_one + vec(V_SHIFT1, 6)
        hidden[...] = value
        hidden_low[...] = value.astype(BF16)
        hidden_t[...] = value.astype(BF16).T

        in_waves(arrivals, read_first, False, lambda copy: copy.wait())

        def up_step(tile, carry):
            pre = nn(hidden_low[...], load_wide(UP, 2 * tile, 2)) + vec(V_UP + 2 * tile, 2)
            below = 0.5 * (1.0 + lax.erf(pre * (0.5**0.5)))
            cols = pl.ds(aligned(tile * 256, 256), 256)
            act[:, cols] = (pre * below).astype(BF16)
            slope[:, cols] = below + pre * (jnp.exp(-0.5 * pre * pre) * (1.0 / math.sqrt(2.0 * math.pi)))
            return carry

        lax.fori_loop(0, 12, up_step, 0)
        for tile in range(3):
            cols = pl.ds(tile * 256, 256)
            value = nn(act[...], load_wide(DOWN, 2 * tile, 2)) + vec(V_DOWN + 2 * tile, 2)
            total[:, cols] = hidden[:, cols] + value

        hat, inverse = norm_parts(total[...])
        gain_two = vec(V_GAIN2, 6)
        output_ref[...] = (hat * gain_two + vec(V_SHIFT2, 6)).astype(BF16)
        d_result = cotangent_ref[...].astype(F32)
        vec_grad(V_GAIN2, d_result * hat)
        vec_grad(V_SHIFT2, d_result)
        value = norm_back(d_result * gain_two, hat, inverse)
        d_hidden[...] = value
        d_down = value.astype(BF16)
        vec_grad(V_DOWN, d_down.astype(F32))

        for tile in range(12):
            low, high = tile * 256, (tile + 1) * 256
            cols = pl.ds(low, 256)
            d_act = nt(d_down, load_wide(DOWN, 0, 6, low, high))
            save_wide(DOWN, 0, nn(act[:, cols].T, d_down), low)
            d_up = (d_act * slope[:, cols]).astype(BF16)
            vec_grad(V_UP + 2 * tile, d_up.astype(F32))
            d_hidden[...] += nt(d_up, load_wide(UP, 2 * tile, 2))
            save_wide(UP, 2 * tile, nn(hidden_t[...], d_up))

        departures = []
        for ref, (blocks, at, length) in zip(grad_refs, grad_parts(index)):
            for i, block in enumerate(range(geo.shards) if blocks is None else blocks):
                source = store.at[block, pl.ds(at, length), :]
                departures.append((block, pltpu.make_async_copy(source, ref.at[i], out_sems.at[len(departures)])))

        def done_first(block):
            late, early = block > geo.attention_blocks, block < geo.vector_blocks
            return early and late if isinstance(block, int) else early & late

        in_waves(departures, done_first, True, lambda copy: copy.start())

        d_out = d_hidden[...]
        hat = hat_one[...]
        vec_grad(V_GAIN1, d_out * hat)
        vec_grad(V_SHIFT1, d_out)
        value = norm_back(d_out * gain_one, hat, inverse_one)
        total[...] = value
        d_attn = value.astype(BF16)
        vec_grad(V_OUT, d_attn.astype(F32))
        d_context = nt(d_attn, load_wide(OUT, 0, 6)).astype(BF16)
        context_t = context[...].T
        for tile in range(3):
            save_wide(OUT, 2 * tile, nn(context_t, d_attn[:, tile * 256 : (tile + 1) * 256]))
        context[...] = d_context

        for seq in range(seqs):
            span = pl.ds(seq * L, L)
            for pair in range(pairs):
                weight = probs[seq * pairs + pair]
                d_pair = context[span, pl.ds(pair * LANES, LANES)]
                query, keys = pair_at(seq, pair, 0), pair_at(seq, pair, 1)
                d_weight = nt(d_pair, split_heads(pair_at(seq, pair, 2)))
                mixed = weight * d_weight
                delta = both([jnp.sum(mixed[:, i * L : (i + 1) * L], axis=1, keepdims=True) for i in range(2)])
                d_scores = (weight * (d_weight - delta)).astype(BF16)
                d_query = nn(d_scores, split_heads(keys)) * scale
                stacked = nn(d_scores.T, query)
                d_key = jnp.where(first_head, stacked[:L], stacked[L:]) * scale
                stacked = nn(weight.astype(BF16).T, d_pair)
                d_value = jnp.where(first_head, stacked[:L], stacked[L:])
                for part, item in enumerate((d_query, d_key, d_value)):
                    d_qkv[span, pl.ds(part * D + pair * LANES, LANES)] = item.astype(BF16)

        rows_t = rows_low[...].T
        for tile in range(9):
            value = d_qkv[:, tile * 256 : (tile + 1) * 256]
            if tile < 3:
                vec_grad(V_Q + 2 * tile, value.astype(F32))
            if tile >= 6:
                vec_grad(V_V + 2 * (tile - 6), value.astype(F32))
            total[...] += nt(value, load_wide(QKV, 2 * tile, 2))
            save_wide(QKV, 2 * tile, nn(rows_t, value))
        d_rows = total[...]
        token_grad_ref[...] = d_rows

        d_time = [jnp.sum(d_rows[seq * L : (seq + 1) * L], axis=0, keepdims=True) for seq in range(seqs)]
        d_time = jnp.concatenate(d_time + [jnp.zeros((sines.shape[0] - seqs, D), F32)], axis=0).astype(BF16)
        vec_grad(V_TIME_OUT, d_time.astype(F32))
        d_time_act = nt(d_time, load_wide(TIME_OUT, 0, 6))
        save_wide(TIME_OUT, 0, nn(time_act.T, d_time))
        d_time_pre = (d_time_act * (time_gate * (1.0 + time_pre * (1.0 - time_gate)))).astype(BF16)
        vec_grad(V_TIME_IN, d_time_pre.astype(F32))
        save_wide(TIME_IN, 0, nn(sines.T, d_time_pre))
        save(VEC, 0, vec_grads[...].astype(BF16))

        in_waves(departures, done_first, False, lambda copy: copy.start())
        in_waves(departures, done_first, True, lambda copy: copy.wait())
        in_waves(departures, done_first, False, lambda copy: copy.wait())

    whole = pl.BlockSpec(memory_space=pltpu.VMEM)
    return pl.pallas_call(
        kernel,
        in_specs=[pl.BlockSpec(memory_space=pltpu.SMEM)] * 2
        + [whole] * 3
        + [pl.BlockSpec(memory_space=pl.ANY)] * count,
        out_specs=[whole] * 2 + [pl.BlockSpec(memory_space=pl.ANY)] * len(grad_shapes),
        out_shape=[
            jax.ShapeDtypeStruct((rows, D), BF16),
            jax.ShapeDtypeStruct((rows, D), F32),
        ]
        + [jax.ShapeDtypeStruct(shape, BF16) for shape in grad_shapes],
        scratch_shapes=[
            pltpu.VMEM((geo.shards, geo.rows, LANES), BF16),
            pltpu.VMEM((VEC_ROWS, LANES), F32),
            pltpu.VMEM((VEC_ROWS, LANES), F32),
            pltpu.VMEM((rows, D), F32),
            pltpu.VMEM((rows, D), BF16),
            pltpu.VMEM((rows, 3 * D), BF16),
            pltpu.VMEM((seqs * pairs, L, 2 * L), F32),
            pltpu.VMEM((rows, D), BF16),
            pltpu.VMEM((rows, D), F32),
            pltpu.VMEM((rows, D), F32),
            pltpu.VMEM((rows, D), BF16),
            pltpu.VMEM((D, rows), BF16),
            pltpu.VMEM((rows, FF), BF16),
            pltpu.VMEM((rows, FF), F32),
            pltpu.VMEM((rows, D), F32),
            pltpu.VMEM((rows, D), F32),
            pltpu.VMEM((rows, 3 * D), BF16),
            pltpu.SemaphoreType.DMA((in_count,)),
            pltpu.SemaphoreType.DMA((out_count,)),
        ],
        compiler_params=pltpu.CompilerParams(vmem_limit_bytes=18 * 2**20 + geo.shards * geo.rows * LANES * 2),
        name="model_step",
    )(where, lengths, tokens, cotangent, sinusoid, *pieces)


def neighbor_quarters(index, replica):
    core = index % 2
    return replica, replica ^ (1 + core), replica ^ (2 - core), replica ^ 3


def small_step(name, body, scalars, inputs, shapes, after):
    def kernel(*refs):
        first, last = len(scalars), len(scalars) + len(inputs)
        body(refs[:first], refs[first:last], refs[last + len(after) : -1])
        refs[-1][...] = jnp.zeros(TOKEN, F32)

    whole = pl.BlockSpec(memory_space=pltpu.VMEM)
    return pl.pallas_call(
        kernel,
        in_specs=[pl.BlockSpec(memory_space=pltpu.SMEM)] * len(scalars)
        + [whole] * len(inputs)
        + [pl.BlockSpec(memory_space=pl.ANY)] * len(after),
        out_specs=[whole] * (len(shapes) + 1),
        out_shape=[jax.ShapeDtypeStruct(shape, BF16) for shape in shapes] + [jax.ShapeDtypeStruct(TOKEN, F32)],
        compiler_params=pltpu.CompilerParams(vmem_limit_bytes=12 * 2**20),
        name=name,
    )(*scalars, *inputs, *after)


def stack_up(after, items):
    def body(scalars, inputs, outs):
        at = 0
        for ref in inputs:
            outs[0][pl.ds(at, ref.shape[0]), :] = ref[...]
            at += ref.shape[0]

    return small_step("stack_up", body, [], items, [(sum(item.shape[0] for item in items), LANES)], after)


def join_block(geo, where, after, quarters):
    def body(scalars, inputs, outs):
        for ref, quarter in zip(inputs, neighbor_quarters(scalars[0][0], scalars[0][1])):
            outs[0][pl.ds(aligned(quarter * geo.quarter), geo.quarter), :] = ref[...]

    return small_step("join_block", body, [where], quarters, [(geo.rows, LANES)], after)


def reduce_step(geo, where, after, cores=None, pair=None, items=None, head=None, tails=None, halves=False):
    size = geo.quarter
    inputs, shapes = [], []
    if cores is not None:
        inputs += cores + [tails] * (tails is not None)
        shapes += [(2, head or size, LANES)] * 2 + [(4 * (size - (head or 0)), LANES)] * (head is not None)
    if pair is not None:
        inputs += pair
        rows = pair[0].shape[1]
        shapes += [(rows // 2, LANES)] * 4 if halves else [(rows, LANES)] * 2
    if items is not None:
        inputs += items
        rows = items[0].shape[0]
        shapes += [(rows // 2, LANES)] * 2 if halves else [(rows, LANES)]

    def body(scalars, inputs, outs):
        inputs, outs = list(inputs), list(outs)

        def save(value):
            start = 0
            while start < value.shape[0]:
                out = outs.pop(0)
                out[...] = value[start : start + out.shape[0], :].astype(BF16)
                start += out.shape[0]

        if cores is not None:
            keep, got = inputs[:2]
            for i, quarter in enumerate(neighbor_quarters(scalars[0][0], scalars[0][1])):
                span = pl.ds(aligned(quarter * size), head or size)
                value = keep[span, :].astype(F32) + got[span, :].astype(F32)
                if tails is not None:
                    more = inputs[2].shape[0] // 4
                    tail = inputs[2][pl.ds(aligned(quarter * more), more), :].astype(F32)
                    value = jnp.concatenate([value[: size - more], value[size - more :] + tail], axis=0)
                outs[i // 2][i % 2] = value.astype(BF16)
            if head is not None:
                more = size - head
                for i in range(4):
                    span = pl.ds(i * size + head, more)
                    value = keep[span, :].astype(F32) + got[span, :].astype(F32)
                    outs[2][pl.ds(i * more, more), :] = value.astype(BF16)
            inputs = inputs[2 + (tails is not None) :]
            del outs[: 2 + (head is not None)]
        if pair is not None:
            near, got = inputs[:2]
            for i in range(2):
                save(near[i].astype(F32) + got[i].astype(F32))
            inputs = inputs[2:]
        if items is not None:
            edges = sorted({0} | {ref.shape[0] for ref in inputs})
            values = []
            for low, high in zip(edges, edges[1:]):
                parts = [ref[pl.ds(low, high - low), :].astype(F32) for ref in inputs if ref.shape[0] > low]
                values.append(sum(parts[1:], parts[0]))
            save(values[0] if len(values) == 1 else jnp.concatenate(values, axis=0))

    return small_step("reduce_step", body, [where], inputs, shapes, after)


def ring_order(size):
    return list(range(0, size, 2))[:1] + list(range(1, size, 2)) + list(range(size - 2, 0, -2))


def select(value, choices):
    out = jnp.int32(choices[0])
    for i, choice in enumerate(choices[1:], 1):
        out = jnp.where(value == i, choice, out)
    return out


def make_local(dp, fsdp):
    direct_links = dp == 4 and fsdp == 8
    chips = fsdp // 2
    order = ring_order(chips)
    before = [order[order.index(chip) - 1] for chip in range(chips)]

    def chip_before(chip, hops):
        table = list(range(chips))
        for _ in range(hops):
            table = [before[item] for item in table]
        return select(chip, table)

    def permute(value, axes, target):
        pairs = []
        for replica in range(dp):
            for index in range(fsdp):
                pairs.append((replica * fsdp + index, target(replica, index)))
        return lax.ppermute(value, axes, pairs)

    def core_swap(value):
        return lax.ppermute(value, "fsdp", [(index, index ^ 1) for index in range(fsdp)])

    def ring_hop(value, hops=1):
        pairs = []
        for place, chip in enumerate(order):
            target = order[(place + hops) % chips]
            pairs += [(chip * 2 + core, target * 2 + core) for core in range(2)]
        return lax.ppermute(value, "fsdp", pairs)

    def first_way(value):
        return permute(value, ("dp", "fsdp"), lambda r, i: (r ^ (1 + i % 2)) * fsdp + i)

    def second_way(value):
        return permute(value, ("dp", "fsdp"), lambda r, i: (r ^ (2 - i % 2)) * fsdp + i)

    def local(tokens, lengths, timesteps, cotangent, params, moment_one, moment_two):
        geo = Geometry(params.shape[0] * fsdp, fsdp)
        where = jnp.stack([lax.axis_index("fsdp"), lax.axis_index("dp")]).astype(jnp.int32)
        seqs = tokens.shape[0]

        half_freq = TFREQ // 2
        frequencies = jnp.exp(-math.log(10000.0) * jnp.arange(half_freq, dtype=F32) / half_freq)
        angles = timesteps.astype(F32)[:, None] * frequencies[None, :]
        sinusoid = jnp.concatenate([jnp.cos(angles), jnp.sin(angles)], axis=1).astype(BF16)
        sinusoid = jnp.pad(sinusoid, ((0, up_to(seqs, ROUND) - seqs), (0, 0)))

        block, quarter = pack_block(geo, params, where)

        def block_of(hops, other=0):
            return lambda index: chip_before(index // 2, hops) * 2 + (index % 2 ^ other)

        if direct_links:
            swapped = core_swap(block)
            pieces = [block, swapped]
            quarter_1, token = stack_up([], [ring_hop(quarter)])
            hop, one_1, two_1 = ring_hop(quarter_1), first_way(quarter_1), second_way(quarter_1)
            quarter_2, token = stack_up([token, swapped], [hop])
            hop, one_2, two_2 = ring_hop(quarter_2), first_way(quarter_2), second_way(quarter_2)
            passed, token = stack_up([token, two_1], [one_1])
            three_1 = second_way(passed)
            quarter_3, token = stack_up([token], [hop])
            one_3, two_3 = first_way(quarter_3), second_way(quarter_3)
            passed, token = stack_up([token, two_2], [one_2])
            three_2 = second_way(passed)
            block, token = join_block(geo, where, [token], [quarter_1, one_1, two_1, three_1])
            swapped = core_swap(block)
            pieces += [block, swapped]
            passed, token = stack_up([token, two_3], [one_3])
            three_3 = second_way(passed)
            stack, token = stack_up([token], [quarter_2, one_2, two_2, quarter_3, one_3, two_3])
            stack_swapped = core_swap(stack)
            pieces += [stack, stack_swapped]
            last_2, token = stack_up([token], [three_2])
            last_3, token = stack_up([token, swapped, stack_swapped], [three_3])
            for item in (last_2, last_3):
                pieces += [item, core_swap(item)]

            def weight_places(index, replica):
                places = []
                for hops in range(2):
                    for other in range(2):
                        places.append([(block_of(hops, other)(index), 0, geo.rows, 0)])
                size = geo.quarter
                for which in ((0, 2), (1, 2), (2, 2), (0, 3), (1, 3), (2, 3)), ((3, 2),), ((3, 3),):
                    for other in range(2):
                        quarters = neighbor_quarters(index ^ other, replica)
                        places.append([
                            (block_of(hops, other)(index), i * size, size, quarters[quarter] * size)
                            for i, (quarter, hops) in enumerate(which)
                        ])
                return places

            def grad_parts(index):
                kept = [block_of(hops)(index) for hops in range(1, chips + 1)]
                sent = [block_of(hops, 1)(index) for hops in range(1, chips + 1)]
                return [([block], 0, geo.rows) for block in kept + sent]

        else:
            pieces = [lax.all_gather(block, "fsdp", axis=0)]

            def weight_places(index, replica):
                return [0]

            def grad_parts(index):
                return [(None, 0, geo.rows)]

        output, token_grad, *grads = model_step(
            geo,
            tokens.reshape(seqs * L, D),
            cotangent.reshape(seqs * L, D),
            lengths,
            sinusoid,
            where,
            pieces,
            weight_places,
            grad_parts,
        )

        if direct_links:
            grads = [item[0] for item in grads]
            cores = [[grads[hops], core_swap(grads[chips + hops])] for hops in range(chips)]
            near_1, far_1, tails, token = reduce_step(geo, where, [], cores=cores[0], head=geo.head)
            far_1, tails = second_way(far_1), ring_hop(tails, -1)
            near_2, far_2, token = reduce_step(geo, where, [token], cores=cores[1])
            far_2 = second_way(far_2)
            near_3, far_3, own_1, next_1, token = reduce_step(geo, where, [token], cores=cores[2], pair=[near_1, far_1])
            next_1, far_3 = first_way(next_1), second_way(far_3)
            quarter, token = reduce_step(geo, where, [token], items=[own_1, next_1])
            passed = ring_hop(quarter)
            near_4, far_4, own_2, next_2, token = reduce_step(
                geo, where, [token], cores=cores[3], pair=[near_2, far_2], tails=tails
            )
            next_2, far_4 = first_way(next_2), second_way(far_4)
            own_3, next_3, token = reduce_step(geo, where, [token], pair=[near_3, far_3])
            next_3 = first_way(next_3)
            quarter, token = reduce_step(geo, where, [token], items=[own_2, next_2, passed])
            passed = ring_hop(quarter)
            own_a, own_b, next_a, next_b, token = reduce_step(geo, where, [token], pair=[near_4, far_4], halves=True)
            next_a, next_b = first_way(next_a), first_way(next_b)
            passed_a, passed_b, token = reduce_step(geo, where, [token], items=[own_3, next_3, passed], halves=True)
            passed_a, passed_b = ring_hop(passed_a), ring_hop(passed_b)
            half_a, token = reduce_step(geo, where, [token], items=[own_a, next_a, passed_a])
            one_a, two_a = first_way(half_a), second_way(half_a)
            half_b, token = reduce_step(geo, where, [token], items=[own_b, next_b, passed_b])
            one_b, two_b = first_way(half_b), second_way(half_b)
            pieces = [half_a, half_b, one_a, one_b, two_a, two_b, second_way(one_a), second_way(one_b)]

            def piece_places(index, replica):
                half = geo.quarter // 2
                return [
                    (2 * i + j, 0, half, item * geo.quarter + j * half)
                    for i, item in enumerate(neighbor_quarters(index, replica))
                    for j in range(2)
                ]

        else:
            mine = lax.psum_scatter(grads[0], "fsdp", scatter_dimension=0)
            pieces = [lax.psum(mine, "dp")]

            def piece_places(index, replica):
                return [(0, 0, geo.rows, 0)]

        new_params, new_one, new_two = optimizer_step(
            geo, params, moment_one, moment_two, where, pieces, piece_places
        )
        return (
            output.reshape(tokens.shape),
            token_grad.reshape(tokens.shape),
            new_params,
            new_one,
            new_two,
        )

    return local


def solution(mesh):
    batch = P(("dp", "fsdp"))
    rows = P(("dp", "fsdp"), None, None)
    flat = P("fsdp")
    return jax.shard_map(
        make_local(mesh.shape["dp"], mesh.shape["fsdp"]),
        mesh=mesh,
        in_specs=(rows, batch, batch, rows, flat, flat, flat),
        out_specs=(rows, rows, flat, flat, flat),
        check_vma=False,
    )
```

```python
import math

import jax
import jax.numpy as jnp
from jax import lax
from jax.experimental import pallas as pl
from jax.experimental.pallas import tpu as pltpu
from jax.sharding import PartitionSpec as P

D = 768
HEADS = 12
HEAD_DIM = 64
FF = 3072
TFREQ = 128
THID = 512
STEP = 10
MATS = 7536640
L = 128

NORM_EPS = 1e-05
ADAM_EPS = 1e-08
BETA_ONE = 0.5
BETA_TWO = 0.5
RATE_MATRIX = 0.02
RATE_SMALL = 0.2
WEIGHT_DECAY = 0.01

LANES = 128
ROUND = 16

TIME_IN, TIME_OUT, QKV, OUT, UP, DOWN, VEC = range(7)
MATRICES = [(TFREQ, THID), (THID, D), (D, 3 * D), (D, D), (D, FF), (FF, D), (82, LANES)]
VEC_ROWS = 96
V_TIME_IN, V_TIME_OUT, V_Q, V_V, V_OUT, V_GAIN1, V_SHIFT1, V_UP, V_DOWN, V_GAIN2, V_SHIFT2 = (
    0, 4, 10, 16, 22, 28, 34, 40, 64, 70, 76,
)

F32 = jnp.float32
BF16 = jnp.bfloat16
TOKEN = (8, LANES)
HEAD = 0.50


def up_to(value, step):
    return -(-value // step) * step


class Geometry:
    def __init__(self, total, shards):
        self.shards = shards
        self.length = total // shards
        self.offsets = []
        offset = 0
        for rows, cols in MATRICES:
            self.offsets.append(offset)
            offset += rows * cols
        assert offset == total and total % shards == 0
        self.regions = []
        for index in range(shards):
            low, high = index * self.length, (index + 1) * self.length
            base, found = 0, []
            for matrix, (rows, cols) in enumerate(MATRICES):
                start, stop = max(low, self.offsets[matrix]), min(high, self.offsets[matrix] + rows * cols)
                if start >= stop:
                    continue
                first = (start - self.offsets[matrix]) // cols // ROUND * ROUND
                last = up_to(up_to(stop - self.offsets[matrix], cols) // cols, ROUND)
                found.append((matrix, first, last, base))
                base += (last - first) * (cols // LANES)
            self.regions.append(found)
        used = [
            sum((last - first) * (MATRICES[matrix][1] // LANES) for matrix, first, last, _ in found)
            for found in self.regions
        ]
        self.rows = up_to(max(used), 8 * ROUND)
        self.quarter = self.rows // 4
        self.head = up_to(int(self.quarter * HEAD), ROUND)
        self.runs = []
        for matrix, (rows, cols) in enumerate(MATRICES):
            groups = []
            for group in range(up_to(rows, ROUND) // ROUND):
                row = group * ROUND
                places = []
                for index, found in enumerate(self.regions):
                    for which, first, last, base in found:
                        if which == matrix and first <= row < last:
                            places.append((index, first, last, base))
                assert places
                groups.append((row, places))
            runs = []
            for row, places in groups:
                if runs and runs[-1][2] == places:
                    runs[-1][1] = row + ROUND
                else:
                    runs.append([row, row + ROUND, places])
            self.runs.append([tuple(run) for run in runs])
        self.attention_blocks = max(i for i, found in enumerate(self.regions) if found[0][0] < UP)
        self.vector_blocks = min(i for i, found in enumerate(self.regions) if found[-1][0] == VEC)
        self.margin = ROUND * (FF // LANES)
        self.flat_rows = up_to(up_to(self.length, LANES) // LANES + 1, 8)
        self.buffer_rows = self.margin + self.flat_rows + self.margin + 8

    def table(self):
        out = []
        for index, found in enumerate(self.regions):
            line = [[0, 0, 0] for _ in MATRICES]
            first_row = index * self.length // LANES
            for matrix, first, last, base in found:
                width = MATRICES[matrix][1] // LANES
                start = self.offsets[matrix] // LANES + first * width - first_row + self.margin
                line[matrix] = [start, (last - first) // ROUND, base]
            out.extend(value for item in line for value in item)
        return jnp.array(out, jnp.int32)


def aligned(value, step=ROUND):
    return value if isinstance(value, int) else pl.multiple_of(value, step)


def spread_steps(length):
    steps = 4
    return steps, up_to(-(-length // steps), 8 * 1024)


def region_loop(table, index, body):
    for matrix, (_, cols) in enumerate(MATRICES):
        width = cols // LANES
        at = (index * len(MATRICES) + matrix) * 3
        start, groups, base = table[at], table[at + 1], table[at + 2]

        def group_step(group, carry, width=width, start=start, groups=groups, base=base):
            for column in range(width):
                flat = start + group * (ROUND * width) + column
                place = pl.multiple_of(base + (column * groups + group) * ROUND, ROUND)
                body(flat, width, place)
            return carry

        lax.fori_loop(0, groups, group_step, 0)


def pack_block(geo, params, where):
    steps, chunk = spread_steps(geo.length)
    rows = chunk // LANES

    def kernel(where_ref, table_ref, params_ref, block_ref, quarter_ref, buffer):
        step = pl.program_id(0)
        index = where_ref[0]
        shift = (index * geo.length) % LANES

        @pl.when(step == 0)
        def _():
            buffer[pl.ds(0, geo.margin), :] = jnp.zeros((geo.margin, LANES), F32)
            tail = geo.margin + geo.flat_rows - 8
            rest = buffer.shape[0] - tail
            buffer[pl.ds(tail, rest), :] = jnp.zeros((rest, LANES), F32)

        place = lax.broadcasted_iota(jnp.int32, (64, LANES), 0) * LANES + lax.broadcasted_iota(
            jnp.int32, (64, LANES), 1
        )

        def roll_in(part, carry):
            value = params_ref[pl.ds(pl.multiple_of(part * 8192, 8192), 8192)].reshape(64, LANES)
            before = step * chunk + part * 8192
            value = jnp.where(place + before < geo.length, value, 0.0)
            at = pl.multiple_of(geo.margin + step * rows + part * 64, 8)
            buffer[pl.ds(at, 64), :] = pltpu.roll(value, shift, 1)
            return carry

        lax.fori_loop(0, chunk // 8192, roll_in, 0, unroll=True)

        @pl.when(step == steps - 1)
        def _():
            late = lax.broadcasted_iota(jnp.int32, (ROUND, LANES), 1) >= shift

            def move(flat, width, place):
                here = buffer[pl.ds(flat, ROUND, stride=width), :]
                above = buffer[pl.ds(flat - 1, ROUND, stride=width), :]
                block_ref[pl.ds(place, ROUND), :] = jnp.where(late, here, above).astype(BF16)

            region_loop(table_ref, index, move)
            mine = pl.multiple_of(where_ref[1] * geo.quarter, ROUND)
            quarter_ref[...] = block_ref[pl.ds(mine, geo.quarter), :]

    buffer_rows = geo.margin + max(steps * rows, geo.flat_rows) + geo.margin + 8
    sizes = [geo.rows, geo.quarter]
    return pl.pallas_call(
        kernel,
        grid=(steps,),
        in_specs=[
            pl.BlockSpec(memory_space=pltpu.SMEM),
            pl.BlockSpec(memory_space=pltpu.SMEM),
            pl.BlockSpec((chunk,), lambda i: (i,)),
        ],
        out_specs=[pl.BlockSpec(memory_space=pltpu.VMEM)] * len(sizes),
        out_shape=[jax.ShapeDtypeStruct((size, LANES), BF16) for size in sizes],
        scratch_shapes=[pltpu.VMEM((buffer_rows, LANES), F32)],
        compiler_params=pltpu.CompilerParams(vmem_limit_bytes=16 * 2**20),
        name="pack_block",
    )(where, geo.table(), params)


def optimizer_step(geo, params, moment_one, moment_two, where, pieces, piece_places):
    steps, chunk = spread_steps(geo.length)
    rows = chunk // LANES
    count = len(pieces)
    corr_one = 1.0 - BETA_ONE**STEP
    corr_two = 1.0 - BETA_TWO**STEP

    def kernel(where_ref, table_ref, *refs):
        piece_refs = refs[:count]
        params_ref, one_ref, two_ref, new_params_ref, new_one_ref, new_two_ref, block, buffer = refs[count:]
        step = pl.program_id(0)
        index = where_ref[0]
        shift = (index * geo.length) % LANES

        @pl.when(step == 0)
        def _():
            for piece, start, length, at in piece_places(index, where_ref[1]):
                block[pl.ds(aligned(at), length), :] = piece_refs[piece][pl.ds(start, length), :]

            def move(flat, width, place):
                buffer[pl.ds(flat, ROUND, stride=width), :] = block[pl.ds(place, ROUND), :].astype(F32)

            region_loop(table_ref, index, move)

        late = lax.broadcasted_iota(jnp.int32, (64, LANES), 1) >= shift
        place = lax.broadcasted_iota(jnp.int32, (64, LANES), 0) * LANES + lax.broadcasted_iota(
            jnp.int32, (64, LANES), 1
        )

        def update(part, carry):
            at = geo.margin + step * rows + part * 64
            here = buffer[pl.ds(pl.multiple_of(at, 8), 64), :]
            below = buffer[pl.ds(at + 1, 64), :]
            grad = pltpu.roll(jnp.where(late, here, below), LANES - shift, 1)
            span = pl.ds(pl.multiple_of(part * 8192, 8192), 8192)
            old = params_ref[span].reshape(64, LANES)
            new_one = BETA_ONE * one_ref[span].reshape(64, LANES) + (1.0 - BETA_ONE) * grad
            new_two = BETA_TWO * two_ref[span].reshape(64, LANES) + (1.0 - BETA_TWO) * grad * grad
            is_matrix = place + (index * geo.length + step * chunk + part * 8192) < MATS
            rates = jnp.where(is_matrix, RATE_MATRIX, RATE_SMALL)
            decays = jnp.where(is_matrix, WEIGHT_DECAY, 0.0)
            change = new_one / corr_one / (jnp.sqrt(new_two / corr_two) + ADAM_EPS)
            new_params_ref[span] = (old - rates * (change + decays * old)).reshape(8192)
            new_one_ref[span] = new_one.reshape(8192)
            new_two_ref[span] = new_two.reshape(8192)
            return carry

        lax.fori_loop(0, chunk // 8192, update, 0, unroll=True)

    buffer_rows = geo.margin + max(steps * rows, geo.flat_rows) + geo.margin + 8
    flat_spec = pl.BlockSpec((chunk,), lambda i: (i,))
    flat_shape = jax.ShapeDtypeStruct((geo.length,), F32)
    return pl.pallas_call(
        kernel,
        grid=(steps,),
        in_specs=[pl.BlockSpec(memory_space=pltpu.SMEM)] * 2
        + [pl.BlockSpec(memory_space=pltpu.VMEM)] * count
        + [flat_spec] * 3,
        out_specs=[flat_spec] * 3,
        out_shape=[flat_shape] * 3,
        scratch_shapes=[
            pltpu.VMEM((geo.rows, LANES), BF16),
            pltpu.VMEM((buffer_rows, LANES), F32),
        ],
        compiler_params=pltpu.CompilerParams(vmem_limit_bytes=24 * 2**20),
        name="optimizer_step",
    )(where, geo.table(), *pieces, params, moment_one, moment_two)


def nn(left, right):
    return lax.dot_general(left, right, (((1,), (0,)), ((), ())), preferred_element_type=F32)


def nt(left, right):
    return lax.dot_general(left, right, (((1,), (1,)), ((), ())), preferred_element_type=F32)


def norm_parts(values):
    center = values - jnp.mean(values, axis=-1, keepdims=True)
    inverse = lax.rsqrt(jnp.mean(center * center, axis=-1, keepdims=True) + NORM_EPS)
    return center * inverse, inverse


def norm_back(scaled, hat, inverse):
    return inverse * (
        scaled
        - jnp.mean(scaled, axis=-1, keepdims=True)
        - hat * jnp.mean(scaled * hat, axis=-1, keepdims=True)
    )


def model_step(geo, tokens, cotangent, lengths, sinusoid, where, pieces, piece_places, grad_parts):
    seqs = tokens.shape[0] // L
    rows = tokens.shape[0]
    count = len(pieces)
    pairs = HEADS // 2
    scale = HEAD_DIM ** (-0.5)
    grad_shapes = [
        ((geo.shards if blocks is None else len(blocks), length, LANES)) for blocks, _, length in grad_parts(0)
    ]
    in_count = sum(geo.shards if isinstance(runs, int) else len(runs) for runs in piece_places(0, 0))
    out_count = sum(shape[0] for shape in grad_shapes)
    half = len(grad_shapes) // 2
    near_grads = [half > 0 and i % half < 1 for i in range(len(grad_shapes))]

    def kernel(where_ref, lengths_ref, tokens_ref, cotangent_ref, sinusoid_ref, *refs):
        piece_refs = refs[:count]
        refs = refs[count:]
        output_ref, token_grad_ref = refs[:2]
        grad_refs = refs[2 : 2 + len(grad_shapes)]
        (
            store, vecs, vec_grads, rows_zero, rows_low, qkv, probs, context, hat_one, hidden, hidden_low, hidden_t,
            act, slope, total, d_hidden, d_qkv, in_sems, out_sems,
        ) = refs[2 + len(grad_shapes) :]

        index, replica = where_ref[0], where_ref[1]

        def in_waves(copies, is_early, early, act):
            for block, copy in copies:
                now = is_early(block)
                if isinstance(block, int):
                    if early == now:
                        act(copy)
                else:
                    pl.when(now if early else jnp.logical_not(now))(lambda copy=copy: act(copy))

        arrivals = []
        for ref, runs in zip(piece_refs, piece_places(index, replica)):
            if isinstance(runs, int):
                runs = [(block, None, ref.shape[1], runs) for block in range(geo.shards)]
            for block, start, length, at in runs:
                if start is not None and ref.shape[0] < geo.rows:
                    store[block, pl.ds(aligned(at), length), :] = ref[pl.ds(start, length), :]
                    continue
                source = ref.at[block] if start is None else ref.at[pl.ds(start, length), :]
                target = store.at[block, pl.ds(aligned(at), length), :]
                arrivals.append((block, pltpu.make_async_copy(source, target, in_sems.at[len(arrivals)])))
                arrivals[-1][1].start()

        def read_first(block):
            early, late = block <= geo.attention_blocks, block >= geo.vector_blocks
            return early or late if isinstance(block, int) else early | late

        in_waves(arrivals, read_first, True, lambda copy: copy.wait())

        def spans(matrix, low, high):
            for first, last, places in geo.runs[matrix]:
                start, stop = max(first, low), min(last, high)
                if start < stop:
                    yield start, stop, places

        def ref_rows(place, column, start, stop):
            block, first, last, base = place
            at = base + column * (last - first) + start - first
            return store.at[block, pl.ds(aligned(at), stop - start), :]

        def load(matrix, column, low=0, high=None):
            parts = []
            for start, stop, places in spans(matrix, low, high or up_to(MATRICES[matrix][0], ROUND)):
                value = ref_rows(places[0], column, start, stop)[...]
                for place in places[1:]:
                    value = value + ref_rows(place, column, start, stop)[...]
                parts.append(value)
            return parts[0] if len(parts) == 1 else jnp.concatenate(parts, axis=0)

        def load_wide(matrix, column, wide, low=0, high=None):
            return jnp.concatenate([load(matrix, column + i, low, high) for i in range(wide)], axis=1)

        def save(matrix, column, value, low=0):
            for start, stop, places in spans(matrix, low, low + value.shape[0]):
                for place in places:
                    ref_rows(place, column, start, stop)[...] = value[start - low : stop - low, :]

        def save_wide(matrix, column, value, low=0):
            value = value.astype(BF16)
            for i in range(value.shape[1] // LANES):
                save(matrix, column + i, value[:, i * LANES : (i + 1) * LANES], low)

        def vec(row, wide):
            return jnp.concatenate([vecs[pl.ds(row + i, 1), :] for i in range(wide)], axis=1)

        def vec_grad(row, value):
            sums = jnp.sum(value, axis=0, keepdims=True)
            for i in range(sums.shape[1] // LANES):
                vec_grads[pl.ds(row + i, 1), :] = sums[:, i * LANES : (i + 1) * LANES]

        vecs[...] = load(VEC, 0).astype(F32)
        vec_grads[...] = jnp.zeros((VEC_ROWS, LANES), F32)

        sines = sinusoid_ref[...]
        time_pre = nn(sines, load_wide(TIME_IN, 0, 4)) + vec(V_TIME_IN, 4)
        time_gate = 1.0 / (1.0 + jnp.exp(-time_pre))
        time_act = (time_pre * time_gate).astype(BF16)
        time_emb = nn(time_act, load_wide(TIME_OUT, 0, 6)) + vec(V_TIME_OUT, 6)
        for seq in range(seqs):
            span = pl.ds(seq * L, L)
            value = tokens_ref[span, :].astype(F32) + time_emb[seq : seq + 1, :]
            rows_zero[span, :] = value
            rows_low[span, :] = value.astype(BF16)

        for tile in range(9):
            value = nn(rows_low[...], load_wide(QKV, 2 * tile, 2))
            if tile < 3:
                value = value + vec(V_Q + 2 * tile, 2)
            if tile >= 6:
                value = value + vec(V_V + 2 * (tile - 6), 2)
            qkv[:, tile * 256 : (tile + 1) * 256] = value.astype(BF16)

        first_head = lax.broadcasted_iota(jnp.int32, (L, LANES), 1) < HEAD_DIM

        def split_heads(value):
            zero = jnp.zeros_like(value)
            return jnp.concatenate([jnp.where(first_head, value, zero), jnp.where(first_head, zero, value)], axis=0)

        def both(value):
            return jnp.concatenate([jnp.broadcast_to(item, (L, L)) for item in value], axis=1)

        def pair_at(seq, pair, part):
            return qkv[pl.ds(seq * L, L), pl.ds(part * D + pair * LANES, LANES)]

        key = lax.broadcasted_iota(jnp.int32, (L, 2 * L), 1) % L
        for seq in range(seqs):
            valid = key < lengths_ref[seq]
            for pair in range(pairs):
                scores = nt(pair_at(seq, pair, 0), split_heads(pair_at(seq, pair, 1))) * scale
                scores = jnp.where(valid, scores, -1e30)
                top = both([jnp.max(scores[:, i * L : (i + 1) * L], axis=1, keepdims=True) for i in range(2)])
                power = jnp.exp(scores - top)
                sums = [jnp.sum(power[:, i * L : (i + 1) * L], axis=1, keepdims=True) for i in range(2)]
                weight = power * both([1.0 / item for item in sums])
                probs[seq * pairs + pair] = weight
                value = nn(weight.astype(BF16), split_heads(pair_at(seq, pair, 2)))
                context[pl.ds(seq * L, L), pl.ds(pair * LANES, LANES)] = value.astype(BF16)

        for tile in range(3):
            cols = pl.ds(tile * 256, 256)
            value = nn(context[...], load_wide(OUT, 2 * tile, 2)) + vec(V_OUT + 2 * tile, 2)
            total[:, cols] = rows_zero[:, cols] + value
        hat, inverse_one = norm_parts(total[...])
        hat_one[...] = hat
        gain_one = vec(V_GAIN1, 6)
        value = hat * gain_one + vec(V_SHIFT1, 6)
        hidden[...] = value
        hidden_low[...] = value.astype(BF16)
        hidden_t[...] = value.astype(BF16).T

        in_waves(arrivals, read_first, False, lambda copy: copy.wait())

        def up_step(tile, carry):
            pre = nn(hidden_low[...], load_wide(UP, 2 * tile, 2)) + vec(V_UP + 2 * tile, 2)
            below = 0.5 * (1.0 + lax.erf(pre * (0.5**0.5)))
            cols = pl.ds(aligned(tile * 256, 256), 256)
            act[:, cols] = (pre * below).astype(BF16)
            slope[:, cols] = below + pre * (jnp.exp(-0.5 * pre * pre) * (1.0 / math.sqrt(2.0 * math.pi)))
            return carry

        lax.fori_loop(0, 12, up_step, 0)
        for tile in range(3):
            cols = pl.ds(tile * 256, 256)
            value = nn(act[...], load_wide(DOWN, 2 * tile, 2)) + vec(V_DOWN + 2 * tile, 2)
            total[:, cols] = hidden[:, cols] + value

        hat, inverse = norm_parts(total[...])
        gain_two = vec(V_GAIN2, 6)
        output_ref[...] = (hat * gain_two + vec(V_SHIFT2, 6)).astype(BF16)
        d_result = cotangent_ref[...].astype(F32)
        vec_grad(V_GAIN2, d_result * hat)
        vec_grad(V_SHIFT2, d_result)
        value = norm_back(d_result * gain_two, hat, inverse)
        d_hidden[...] = value
        d_down = value.astype(BF16)
        vec_grad(V_DOWN, d_down.astype(F32))

        for tile in range(12):
            low, high = tile * 256, (tile + 1) * 256
            cols = pl.ds(low, 256)
            d_act = nt(d_down, load_wide(DOWN, 0, 6, low, high))
            save_wide(DOWN, 0, nn(act[:, cols].T, d_down), low)
            d_up = (d_act * slope[:, cols]).astype(BF16)
            vec_grad(V_UP + 2 * tile, d_up.astype(F32))
            d_hidden[...] += nt(d_up, load_wide(UP, 2 * tile, 2))
            save_wide(UP, 2 * tile, nn(hidden_t[...], d_up))

        departures, near_refs = [], []
        for near, ref, (blocks, at, length) in zip(near_grads, grad_refs, grad_parts(index)):
            if near:
                near_refs.append((ref, blocks[0]))
                continue
            for i, block in enumerate(range(geo.shards) if blocks is None else blocks):
                source = store.at[block, pl.ds(at, length), :]
                departures.append((block, pltpu.make_async_copy(source, ref.at[i], out_sems.at[len(departures)])))

        def done_first(block):
            late, early = block > geo.attention_blocks, block < geo.vector_blocks
            return early and late if isinstance(block, int) else early & late

        in_waves(departures, done_first, True, lambda copy: copy.start())

        d_out = d_hidden[...]
        hat = hat_one[...]
        vec_grad(V_GAIN1, d_out * hat)
        vec_grad(V_SHIFT1, d_out)
        value = norm_back(d_out * gain_one, hat, inverse_one)
        total[...] = value
        d_attn = value.astype(BF16)
        vec_grad(V_OUT, d_attn.astype(F32))
        d_context = nt(d_attn, load_wide(OUT, 0, 6)).astype(BF16)
        context_t = context[...].T
        for tile in range(3):
            save_wide(OUT, 2 * tile, nn(context_t, d_attn[:, tile * 256 : (tile + 1) * 256]))
        context[...] = d_context

        for seq in range(seqs):
            span = pl.ds(seq * L, L)
            for pair in range(pairs):
                weight = probs[seq * pairs + pair]
                d_pair = context[span, pl.ds(pair * LANES, LANES)]
                query, keys = pair_at(seq, pair, 0), pair_at(seq, pair, 1)
                d_weight = nt(d_pair, split_heads(pair_at(seq, pair, 2)))
                mixed = weight * d_weight
                delta = both([jnp.sum(mixed[:, i * L : (i + 1) * L], axis=1, keepdims=True) for i in range(2)])
                d_scores = (weight * (d_weight - delta)).astype(BF16)
                d_query = nn(d_scores, split_heads(keys)) * scale
                stacked = nn(d_scores.T, query)
                d_key = jnp.where(first_head, stacked[:L], stacked[L:]) * scale
                stacked = nn(weight.astype(BF16).T, d_pair)
                d_value = jnp.where(first_head, stacked[:L], stacked[L:])
                for part, item in enumerate((d_query, d_key, d_value)):
                    d_qkv[span, pl.ds(part * D + pair * LANES, LANES)] = item.astype(BF16)

        rows_t = rows_low[...].T
        for tile in range(9):
            value = d_qkv[:, tile * 256 : (tile + 1) * 256]
            if tile < 3:
                vec_grad(V_Q + 2 * tile, value.astype(F32))
            if tile >= 6:
                vec_grad(V_V + 2 * (tile - 6), value.astype(F32))
            total[...] += nt(value, load_wide(QKV, 2 * tile, 2))
            save_wide(QKV, 2 * tile, nn(rows_t, value))
        d_rows = total[...]
        token_grad_ref[...] = d_rows

        d_time = [jnp.sum(d_rows[seq * L : (seq + 1) * L], axis=0, keepdims=True) for seq in range(seqs)]
        d_time = jnp.concatenate(d_time + [jnp.zeros((sines.shape[0] - seqs, D), F32)], axis=0).astype(BF16)
        vec_grad(V_TIME_OUT, d_time.astype(F32))
        d_time_act = nt(d_time, load_wide(TIME_OUT, 0, 6))
        save_wide(TIME_OUT, 0, nn(time_act.T, d_time))
        d_time_pre = (d_time_act * (time_gate * (1.0 + time_pre * (1.0 - time_gate)))).astype(BF16)
        vec_grad(V_TIME_IN, d_time_pre.astype(F32))
        save_wide(TIME_IN, 0, nn(sines.T, d_time_pre))
        save(VEC, 0, vec_grads[...].astype(BF16))

        in_waves(departures, done_first, False, lambda copy: copy.start())
        for ref, block in near_refs:
            ref[0] = store[block]
        in_waves(departures, done_first, True, lambda copy: copy.wait())
        in_waves(departures, done_first, False, lambda copy: copy.wait())

    whole = pl.BlockSpec(memory_space=pltpu.VMEM)
    return pl.pallas_call(
        kernel,
        in_specs=[pl.BlockSpec(memory_space=pltpu.SMEM)] * 2
        + [whole] * 3
        + [pl.BlockSpec(memory_space=pl.ANY) if item.size >= geo.rows * LANES else whole for item in pieces],
        out_specs=[whole] * 2 + [whole if near else pl.BlockSpec(memory_space=pltpu.HBM) for near in near_grads],
        out_shape=[
            jax.ShapeDtypeStruct((rows, D), BF16),
            jax.ShapeDtypeStruct((rows, D), F32),
        ]
        + [jax.ShapeDtypeStruct(shape, BF16) for shape in grad_shapes],
        scratch_shapes=[
            pltpu.VMEM((geo.shards, geo.rows, LANES), BF16),
            pltpu.VMEM((VEC_ROWS, LANES), F32),
            pltpu.VMEM((VEC_ROWS, LANES), F32),
            pltpu.VMEM((rows, D), F32),
            pltpu.VMEM((rows, D), BF16),
            pltpu.VMEM((rows, 3 * D), BF16),
            pltpu.VMEM((seqs * pairs, L, 2 * L), F32),
            pltpu.VMEM((rows, D), BF16),
            pltpu.VMEM((rows, D), F32),
            pltpu.VMEM((rows, D), F32),
            pltpu.VMEM((rows, D), BF16),
            pltpu.VMEM((D, rows), BF16),
            pltpu.VMEM((rows, FF), BF16),
            pltpu.VMEM((rows, FF), F32),
            pltpu.VMEM((rows, D), F32),
            pltpu.VMEM((rows, D), F32),
            pltpu.VMEM((rows, 3 * D), BF16),
            pltpu.SemaphoreType.DMA((in_count,)),
            pltpu.SemaphoreType.DMA((out_count,)),
        ],
        compiler_params=pltpu.CompilerParams(vmem_limit_bytes=18 * 2**20 + geo.shards * geo.rows * LANES * 2),
        name="model_step",
    )(where, lengths, tokens, cotangent, sinusoid, *pieces)


def neighbor_quarters(index, replica):
    core = index % 2
    return replica, replica ^ (1 + core), replica ^ (2 - core), replica ^ 3


def small_step(name, body, scalars, inputs, shapes, after):
    def kernel(*refs):
        first, last = len(scalars), len(scalars) + len(inputs)
        body(refs[:first], refs[first:last], refs[last + len(after) : -1])
        refs[-1][...] = jnp.zeros(TOKEN, F32)

    whole = pl.BlockSpec(memory_space=pltpu.VMEM)
    return pl.pallas_call(
        kernel,
        in_specs=[pl.BlockSpec(memory_space=pltpu.SMEM)] * len(scalars)
        + [whole] * len(inputs)
        + [pl.BlockSpec(memory_space=pl.ANY)] * len(after),
        out_specs=[whole] * (len(shapes) + 1),
        out_shape=[jax.ShapeDtypeStruct(shape, BF16) for shape in shapes] + [jax.ShapeDtypeStruct(TOKEN, F32)],
        compiler_params=pltpu.CompilerParams(vmem_limit_bytes=12 * 2**20),
        name=name,
    )(*scalars, *inputs, *after)


def stack_up(after, *groups):
    def body(scalars, inputs, outs):
        inputs = list(inputs)
        for group, out in zip(groups, outs):
            at = 0
            for item in group:
                out[pl.ds(at, item.shape[0]), :] = inputs.pop(0)[...]
                at += item.shape[0]

    items = [item for group in groups for item in group]
    shapes = [(sum(item.shape[0] for item in group), LANES) for group in groups]
    return small_step("stack_up", body, [], items, shapes, after)


def reduce_step(geo, where, after, cores=None, pair=None, items=None, head=None, tails=None, halves=False):
    size = geo.quarter
    inputs, shapes = [], []
    if cores is not None:
        inputs += cores + [tails] * (tails is not None)
        shapes += [(2, head or size, LANES)] * 2 + [(4 * (size - (head or 0)), LANES)] * (head is not None)
    if pair is not None:
        inputs += pair
        rows = pair[0].shape[1]
        shapes += [(rows // 2, LANES)] * 4 if halves else [(rows, LANES)] * 2
    if items is not None:
        inputs += items
        rows = items[0].shape[0]
        shapes += [(rows // 2, LANES)] * 2 if halves else [(rows, LANES)]

    def body(scalars, inputs, outs):
        inputs, outs = list(inputs), list(outs)

        def save(value):
            start = 0
            while start < value.shape[0]:
                out = outs.pop(0)
                out[...] = value[start : start + out.shape[0], :].astype(BF16)
                start += out.shape[0]

        if cores is not None:
            keep, got = inputs[:2]
            for i, quarter in enumerate(neighbor_quarters(scalars[0][0], scalars[0][1])):
                span = pl.ds(aligned(quarter * size), head or size)
                value = keep[span, :].astype(F32) + got[span, :].astype(F32)
                if tails is not None:
                    more = inputs[2].shape[0] // 4
                    tail = inputs[2][pl.ds(aligned(quarter * more), more), :].astype(F32)
                    value = jnp.concatenate([value[: size - more], value[size - more :] + tail], axis=0)
                outs[i // 2][i % 2] = value.astype(BF16)
            if head is not None:
                more = size - head
                for i in range(4):
                    span = pl.ds(i * size + head, more)
                    value = keep[span, :].astype(F32) + got[span, :].astype(F32)
                    outs[2][pl.ds(i * more, more), :] = value.astype(BF16)
            inputs = inputs[2 + (tails is not None) :]
            del outs[: 2 + (head is not None)]
        if pair is not None:
            near, got = inputs[:2]
            for i in range(2):
                save(near[i].astype(F32) + got[i].astype(F32))
            inputs = inputs[2:]
        if items is not None:
            edges = sorted({0} | {ref.shape[0] for ref in inputs})
            values = []
            for low, high in zip(edges, edges[1:]):
                parts = [ref[pl.ds(low, high - low), :].astype(F32) for ref in inputs if ref.shape[0] > low]
                values.append(sum(parts[1:], parts[0]))
            save(values[0] if len(values) == 1 else jnp.concatenate(values, axis=0))

    return small_step("reduce_step", body, [where], inputs, shapes, after)


def ring_order(size):
    return list(range(0, size, 2))[:1] + list(range(1, size, 2)) + list(range(size - 2, 0, -2))


def select(value, choices):
    out = jnp.int32(choices[0])
    for i, choice in enumerate(choices[1:], 1):
        out = jnp.where(value == i, choice, out)
    return out


def make_local(dp, fsdp):
    direct_links = dp == 4 and fsdp == 8
    chips = fsdp // 2
    order = ring_order(chips)
    before = [order[order.index(chip) - 1] for chip in range(chips)]

    def chip_before(chip, hops):
        table = list(range(chips))
        for _ in range(hops):
            table = [before[item] for item in table]
        return select(chip, table)

    def permute(value, axes, target):
        pairs = []
        for replica in range(dp):
            for index in range(fsdp):
                pairs.append((replica * fsdp + index, target(replica, index)))
        return lax.ppermute(value, axes, pairs)

    def core_swap(value):
        return lax.ppermute(value, "fsdp", [(index, index ^ 1) for index in range(fsdp)])

    def ring_hop(value, hops=1):
        pairs = []
        for place, chip in enumerate(order):
            target = order[(place + hops) % chips]
            pairs += [(chip * 2 + core, target * 2 + core) for core in range(2)]
        return lax.ppermute(value, "fsdp", pairs)

    def first_way(value):
        return permute(value, ("dp", "fsdp"), lambda r, i: (r ^ (1 + i % 2)) * fsdp + i)

    def second_way(value):
        return permute(value, ("dp", "fsdp"), lambda r, i: (r ^ (2 - i % 2)) * fsdp + i)

    def local(tokens, lengths, timesteps, cotangent, params, moment_one, moment_two):
        geo = Geometry(params.shape[0] * fsdp, fsdp)
        where = jnp.stack([lax.axis_index("fsdp"), lax.axis_index("dp")]).astype(jnp.int32)
        seqs = tokens.shape[0]

        half_freq = TFREQ // 2
        frequencies = jnp.exp(-math.log(10000.0) * jnp.arange(half_freq, dtype=F32) / half_freq)
        angles = timesteps.astype(F32)[:, None] * frequencies[None, :]
        sinusoid = jnp.concatenate([jnp.cos(angles), jnp.sin(angles)], axis=1).astype(BF16)
        sinusoid = jnp.pad(sinusoid, ((0, up_to(seqs, ROUND) - seqs), (0, 0)))

        block, quarter = pack_block(geo, params, where)

        def block_of(hops, other=0):
            return lambda index: chip_before(index // 2, hops) * 2 + (index % 2 ^ other)

        if direct_links:
            swapped = core_swap(block)
            pieces = [block, swapped]

            def swap(item):
                other = core_swap(item)
                pieces.extend([item, other])
                return other

            near_1, token = stack_up([], [ring_hop(quarter)])
            hop, one_1, two_1 = ring_hop(near_1), first_way(near_1), second_way(near_1)
            near_2, pair_1, token = stack_up([token, swapped, swap(near_1), two_1], [hop], [hop, one_1])
            hop, one_2, far_1 = ring_hop(near_2), first_way(near_2), second_way(pair_1)
            near_3, pair_2, token = stack_up([token, swap(two_1), swap(pair_1)], [hop], [hop, one_2])
            one_3, far_2 = first_way(near_3), second_way(pair_2)
            one_3, token = stack_up([token, swap(pair_2)], [one_3])
            three_3 = second_way(one_3)
            for item in (far_1, one_3, far_2, three_3):
                swap(item)

            def weight_places(index, replica):
                size = geo.quarter
                groups = (
                    ((1, 0),),
                    ((1, 2),),
                    ((2, 0), (1, 1)),
                    ((3, 0), (2, 1)),
                    ((2, 2), (1, 3)),
                    ((3, 1),),
                    ((3, 2), (2, 3)),
                    ((3, 3),),
                )
                places = [[(block_of(0, other)(index), 0, geo.rows, 0)] for other in range(2)]
                for group in groups:
                    for other in range(2):
                        quarters = neighbor_quarters(index ^ other, replica)
                        places.append([
                            (block_of(hops, other)(index), i * size, size, quarters[quarter] * size)
                            for i, (hops, quarter) in enumerate(group)
                        ])
                return places

            def grad_parts(index):
                kept = [block_of(hops)(index) for hops in range(1, chips + 1)]
                sent = [block_of(hops, 1)(index) for hops in range(1, chips + 1)]
                return [([block], 0, geo.rows) for block in kept + sent]

        else:
            pieces = [lax.all_gather(block, "fsdp", axis=0)]

            def weight_places(index, replica):
                return [0]

            def grad_parts(index):
                return [(None, 0, geo.rows)]

        output, token_grad, *grads = model_step(
            geo,
            tokens.reshape(seqs * L, D),
            cotangent.reshape(seqs * L, D),
            lengths,
            sinusoid,
            where,
            pieces,
            weight_places,
            grad_parts,
        )

        if direct_links:
            grads = [item[0] for item in grads]
            cores = [[grads[hops], core_swap(grads[chips + hops])] for hops in range(chips)]
            near_1, far_1, tails, token = reduce_step(geo, where, [], cores=cores[0], head=geo.head)
            far_1, tails = second_way(far_1), ring_hop(tails, -1)
            near_2, far_2, token = reduce_step(geo, where, [token], cores=cores[1])
            far_2 = second_way(far_2)
            near_3, far_3, own_1, next_1, token = reduce_step(geo, where, [token], cores=cores[2], pair=[near_1, far_1])
            next_1, far_3 = first_way(next_1), second_way(far_3)
            quarter, token = reduce_step(geo, where, [token], items=[own_1, next_1])
            passed = ring_hop(quarter)
            near_4, far_4, own_2, next_2, token = reduce_step(
                geo, where, [token], cores=cores[3], pair=[near_2, far_2], tails=tails
            )
            next_2, far_4 = first_way(next_2), second_way(far_4)
            own_3, next_3, token = reduce_step(geo, where, [token], pair=[near_3, far_3])
            next_3 = first_way(next_3)
            quarter, token = reduce_step(geo, where, [token], items=[own_2, next_2, passed])
            passed = ring_hop(quarter)
            own_a, own_b, next_a, next_b, token = reduce_step(geo, where, [token], pair=[near_4, far_4], halves=True)
            next_a, next_b = first_way(next_a), first_way(next_b)
            passed_a, passed_b, token = reduce_step(geo, where, [token], items=[own_3, next_3, passed], halves=True)
            passed_a, passed_b = ring_hop(passed_a), ring_hop(passed_b)
            half_a, token = reduce_step(geo, where, [token], items=[own_a, next_a, passed_a])
            one_a, two_a = first_way(half_a), second_way(half_a)
            half_b, token = reduce_step(geo, where, [token], items=[own_b, next_b, passed_b])
            one_b, two_b = first_way(half_b), second_way(half_b)
            pieces = [half_a, half_b, one_a, one_b, two_a, two_b, second_way(one_a), second_way(one_b)]

            def piece_places(index, replica):
                half = geo.quarter // 2
                return [
                    (2 * i + j, 0, half, item * geo.quarter + j * half)
                    for i, item in enumerate(neighbor_quarters(index, replica))
                    for j in range(2)
                ]

        else:
            mine = lax.psum_scatter(grads[0], "fsdp", scatter_dimension=0)
            pieces = [lax.psum(mine, "dp")]

            def piece_places(index, replica):
                return [(0, 0, geo.rows, 0)]

        new_params, new_one, new_two = optimizer_step(
            geo, params, moment_one, moment_two, where, pieces, piece_places
        )
        return (
            output.reshape(tokens.shape),
            token_grad.reshape(tokens.shape),
            new_params,
            new_one,
            new_two,
        )

    return local


def solution(mesh):
    batch = P(("dp", "fsdp"))
    rows = P(("dp", "fsdp"), None, None)
    flat = P("fsdp")
    return jax.shard_map(
        make_local(mesh.shape["dp"], mesh.shape["fsdp"]),
        mesh=mesh,
        in_specs=(rows, batch, batch, rows, flat, flat, flat),
        out_specs=(rows, rows, flat, flat, flat),
        check_vma=False,
    )
```

```python
import math

import jax
import jax.numpy as jnp
from jax import lax
from jax.experimental import pallas as pl
from jax.experimental.pallas import tpu as pltpu
from jax.sharding import PartitionSpec as P

D = 768
HEADS = 12
HEAD_DIM = 64
FF = 3072
TFREQ = 128
THID = 512
STEP = 10
MATS = 7536640
L = 128

NORM_EPS = 1e-05
ADAM_EPS = 1e-08
BETA_ONE = 0.5
BETA_TWO = 0.5
RATE_MATRIX = 0.02
RATE_SMALL = 0.2
WEIGHT_DECAY = 0.01

LANES = 128
ROUND = 16

TIME_IN, TIME_OUT, QKV, OUT, UP, DOWN, VEC = range(7)
MATRICES = [(TFREQ, THID), (THID, D), (D, 3 * D), (D, D), (D, FF), (FF, D), (82, LANES)]
VEC_ROWS = 96
V_TIME_IN, V_TIME_OUT, V_Q, V_V, V_OUT, V_GAIN1, V_SHIFT1, V_UP, V_DOWN, V_GAIN2, V_SHIFT2 = (
    0, 4, 10, 16, 22, 28, 34, 40, 64, 70, 76,
)

F32 = jnp.float32
BF16 = jnp.bfloat16
TOKEN = (8, LANES)
HEAD = 0.50


def up_to(value, step):
    return -(-value // step) * step


class Geometry:
    def __init__(self, total, shards):
        self.shards = shards
        self.length = total // shards
        self.offsets = []
        offset = 0
        for rows, cols in MATRICES:
            self.offsets.append(offset)
            offset += rows * cols
        assert offset == total and total % shards == 0
        self.regions = []
        for index in range(shards):
            low, high = index * self.length, (index + 1) * self.length
            base, found = 0, []
            for matrix, (rows, cols) in enumerate(MATRICES):
                start, stop = max(low, self.offsets[matrix]), min(high, self.offsets[matrix] + rows * cols)
                if start >= stop:
                    continue
                first = (start - self.offsets[matrix]) // cols // ROUND * ROUND
                last = up_to(up_to(stop - self.offsets[matrix], cols) // cols, ROUND)
                found.append((matrix, first, last, base))
                base += (last - first) * (cols // LANES)
            self.regions.append(found)
        used = [
            sum((last - first) * (MATRICES[matrix][1] // LANES) for matrix, first, last, _ in found)
            for found in self.regions
        ]
        self.rows = up_to(max(used), 8 * ROUND)
        self.quarter = self.rows // 4
        self.head = up_to(int(self.quarter * HEAD), ROUND)
        self.runs = []
        for matrix, (rows, cols) in enumerate(MATRICES):
            groups = []
            for group in range(up_to(rows, ROUND) // ROUND):
                row = group * ROUND
                places = []
                for index, found in enumerate(self.regions):
                    for which, first, last, base in found:
                        if which == matrix and first <= row < last:
                            places.append((index, first, last, base))
                assert places
                groups.append((row, places))
            runs = []
            for row, places in groups:
                if runs and runs[-1][2] == places:
                    runs[-1][1] = row + ROUND
                else:
                    runs.append([row, row + ROUND, places])
            self.runs.append([tuple(run) for run in runs])
        self.attention_blocks = max(i for i, found in enumerate(self.regions) if found[0][0] < UP)
        self.vector_blocks = min(i for i, found in enumerate(self.regions) if found[-1][0] == VEC)
        self.margin = ROUND * (FF // LANES)
        self.flat_rows = up_to(up_to(self.length, LANES) // LANES + 1, 8)
        self.buffer_rows = self.margin + self.flat_rows + self.margin + 8


def aligned(value, step=ROUND):
    return value if isinstance(value, int) else pl.multiple_of(value, step)


def spread_steps(length, steps, unit):
    return steps, up_to(-(-length // steps), unit)


def region_loop(geo, index, body):
    low = index * geo.length
    base = jnp.int32(0)
    for (rows, cols), offset in zip(MATRICES, geo.offsets):
        width = cols // LANES
        start = jnp.maximum(low - offset, 0)
        stop = jnp.minimum(low + geo.length - offset, rows * cols)
        there = stop > start
        first = lax.div(start, ROUND * cols)
        groups = jnp.where(there, lax.div(stop + (ROUND * cols - 1), ROUND * cols) - first, 0)
        row = geo.margin + offset // LANES + first * (ROUND * width) - lax.div(low, LANES)

        def group_step(group, carry, width=width, row=row, groups=groups, base=base):
            for column in range(width):
                flat = row + group * (ROUND * width) + column
                place = pl.multiple_of(base + (column * groups + group) * ROUND, ROUND)
                body(flat, width, place)
            return carry

        lax.fori_loop(0, groups, group_step, 0)
        base = base + groups * (ROUND * width)


def pack_block(geo, params, where):
    steps, chunk = spread_steps(geo.length, 4, 8192)
    rows = chunk // LANES

    def kernel(where_ref, params_ref, block_ref, quarter_ref, buffer):
        step = pl.program_id(0)
        index = where_ref[0]
        shift = (index * geo.length) % LANES

        @pl.when(step == 0)
        def _():
            buffer[pl.ds(0, geo.margin), :] = jnp.zeros((geo.margin, LANES), F32)
            tail = geo.margin + geo.flat_rows - 8
            rest = buffer.shape[0] - tail
            buffer[pl.ds(tail, rest), :] = jnp.zeros((rest, LANES), F32)

        place = lax.broadcasted_iota(jnp.int32, (64, LANES), 0) * LANES + lax.broadcasted_iota(
            jnp.int32, (64, LANES), 1
        )

        def roll_in(part, carry):
            value = params_ref[pl.ds(pl.multiple_of(part * 8192, 8192), 8192)].reshape(64, LANES)
            before = step * chunk + part * 8192
            value = jnp.where(place + before < geo.length, value, 0.0)
            at = pl.multiple_of(geo.margin + step * rows + part * 64, 8)
            buffer[pl.ds(at, 64), :] = pltpu.roll(value, shift, 1)
            return carry

        lax.fori_loop(0, chunk // 8192, roll_in, 0, unroll=True)

        @pl.when(step == steps - 1)
        def _():
            late = lax.broadcasted_iota(jnp.int32, (ROUND, LANES), 1) >= shift

            def move(flat, width, place):
                here = buffer[pl.ds(flat, ROUND, stride=width), :]
                above = buffer[pl.ds(flat - 1, ROUND, stride=width), :]
                block_ref[pl.ds(place, ROUND), :] = jnp.where(late, here, above).astype(BF16)

            region_loop(geo, index, move)
            mine = pl.multiple_of(where_ref[1] * geo.quarter, ROUND)
            quarter_ref[...] = block_ref[pl.ds(mine, geo.quarter), :]

    buffer_rows = geo.margin + max(steps * rows, geo.flat_rows) + geo.margin + 8
    sizes = [geo.rows, geo.quarter]
    return pl.pallas_call(
        kernel,
        grid=(steps,),
        in_specs=[
            pl.BlockSpec(memory_space=pltpu.SMEM),
            pl.BlockSpec((chunk,), lambda i: (i,)),
        ],
        out_specs=[pl.BlockSpec(memory_space=pltpu.VMEM)] * len(sizes),
        out_shape=[jax.ShapeDtypeStruct((size, LANES), BF16) for size in sizes],
        scratch_shapes=[pltpu.VMEM((buffer_rows, LANES), F32)],
        compiler_params=pltpu.CompilerParams(vmem_limit_bytes=16 * 2**20),
        name="pack_block",
    )(where, params)


def optimizer_step(geo, params, moment_one, moment_two, where, pieces, piece_places):
    steps, chunk = spread_steps(geo.length, 4, 8192)
    rows = chunk // LANES
    count = len(pieces)
    corr_one = 1.0 - BETA_ONE**STEP
    corr_two = 1.0 - BETA_TWO**STEP

    def kernel(where_ref, *refs):
        piece_refs = refs[:count]
        params_ref, one_ref, two_ref, new_params_ref, new_one_ref, new_two_ref, block, buffer = refs[count:]
        step = pl.program_id(0)
        index = where_ref[0]
        shift = (index * geo.length) % LANES

        @pl.when(step == 0)
        def _():
            for piece, start, length, at in piece_places(index, where_ref[1]):
                block[pl.ds(aligned(at), length), :] = piece_refs[piece][pl.ds(start, length), :]

            def move(flat, width, place):
                buffer[pl.ds(flat, ROUND, stride=width), :] = block[pl.ds(place, ROUND), :].astype(F32)

            region_loop(geo, index, move)

        late = lax.broadcasted_iota(jnp.int32, (64, LANES), 1) >= shift
        place = lax.broadcasted_iota(jnp.int32, (64, LANES), 0) * LANES + lax.broadcasted_iota(
            jnp.int32, (64, LANES), 1
        )

        def update(part, carry):
            at = geo.margin + step * rows + part * 64
            here = buffer[pl.ds(pl.multiple_of(at, 8), 64), :]
            below = buffer[pl.ds(at + 1, 64), :]
            grad = pltpu.roll(jnp.where(late, here, below), LANES - shift, 1)
            span = pl.ds(pl.multiple_of(part * 8192, 8192), 8192)
            old = params_ref[span].reshape(64, LANES)
            new_one = BETA_ONE * one_ref[span].reshape(64, LANES) + (1.0 - BETA_ONE) * grad
            new_two = BETA_TWO * two_ref[span].reshape(64, LANES) + (1.0 - BETA_TWO) * grad * grad
            is_matrix = place + (index * geo.length + step * chunk + part * 8192) < MATS
            rates = jnp.where(is_matrix, RATE_MATRIX, RATE_SMALL)
            decays = jnp.where(is_matrix, WEIGHT_DECAY, 0.0)
            change = new_one / corr_one / (jnp.sqrt(new_two / corr_two) + ADAM_EPS)
            new_params_ref[span] = (old - rates * (change + decays * old)).reshape(8192)
            new_one_ref[span] = new_one.reshape(8192)
            new_two_ref[span] = new_two.reshape(8192)
            return carry

        lax.fori_loop(0, chunk // 8192, update, 0, unroll=True)

    buffer_rows = geo.margin + max(steps * rows, geo.flat_rows) + geo.margin + 8
    flat_spec = pl.BlockSpec((chunk,), lambda i: (i,))
    flat_shape = jax.ShapeDtypeStruct((geo.length,), F32)
    return pl.pallas_call(
        kernel,
        grid=(steps,),
        in_specs=[pl.BlockSpec(memory_space=pltpu.SMEM)]
        + [pl.BlockSpec(memory_space=pltpu.VMEM)] * count
        + [flat_spec] * 3,
        out_specs=[flat_spec] * 3,
        out_shape=[flat_shape] * 3,
        scratch_shapes=[
            pltpu.VMEM((geo.rows, LANES), BF16),
            pltpu.VMEM((buffer_rows, LANES), F32),
        ],
        compiler_params=pltpu.CompilerParams(vmem_limit_bytes=24 * 2**20),
        name="optimizer_step",
    )(where, *pieces, params, moment_one, moment_two)


def nn(left, right):
    return lax.dot_general(left, right, (((1,), (0,)), ((), ())), preferred_element_type=F32)


def nt(left, right):
    return lax.dot_general(left, right, (((1,), (1,)), ((), ())), preferred_element_type=F32)


def norm_parts(values):
    center = values - jnp.mean(values, axis=-1, keepdims=True)
    inverse = lax.rsqrt(jnp.mean(center * center, axis=-1, keepdims=True) + NORM_EPS)
    return center * inverse, inverse


def norm_back(scaled, hat, inverse):
    return inverse * (
        scaled
        - jnp.mean(scaled, axis=-1, keepdims=True)
        - hat * jnp.mean(scaled * hat, axis=-1, keepdims=True)
    )


def model_step(geo, tokens, cotangent, lengths, sinusoid, where, pieces, piece_places, grad_parts):
    seqs = tokens.shape[0] // L
    rows = tokens.shape[0]
    count = len(pieces)
    pairs = HEADS // 2
    scale = HEAD_DIM ** (-0.5)
    grad_shapes = [
        ((geo.shards if blocks is None else len(blocks), length, LANES)) for blocks, _, length in grad_parts(0)
    ]
    in_count = sum(geo.shards if isinstance(runs, int) else len(runs) for runs in piece_places(0, 0))
    out_count = sum(shape[0] for shape in grad_shapes)
    half = len(grad_shapes) // 2
    near_grads = [half > 0 and i % half < 1 for i in range(len(grad_shapes))]

    def kernel(where_ref, lengths_ref, tokens_ref, cotangent_ref, sinusoid_ref, *refs):
        piece_refs = refs[:count]
        refs = refs[count:]
        output_ref, token_grad_ref = refs[:2]
        grad_refs = refs[2 : 2 + len(grad_shapes)]
        (
            store, vecs, vec_grads, rows_zero, rows_low, qkv, probs, context, hat_one, hidden, hidden_low, hidden_t,
            act, slope, total, d_hidden, d_qkv, in_sems, out_sems,
        ) = refs[2 + len(grad_shapes) :]

        index, replica = where_ref[0], where_ref[1]

        def in_waves(copies, is_early, early, act):
            for block, copy in copies:
                now = is_early(block)
                if isinstance(block, int):
                    if early == now:
                        act(copy)
                else:
                    pl.when(now if early else jnp.logical_not(now))(lambda copy=copy: act(copy))

        arrivals = []
        for ref, runs in zip(piece_refs, piece_places(index, replica)):
            if isinstance(runs, int):
                runs = [(block, None, ref.shape[1], runs) for block in range(geo.shards)]
            for block, start, length, at in runs:
                if start is not None and ref.shape[0] < geo.rows:
                    store[block, pl.ds(aligned(at), length), :] = ref[pl.ds(start, length), :]
                    continue
                source = ref.at[block] if start is None else ref.at[pl.ds(start, length), :]
                target = store.at[block, pl.ds(aligned(at), length), :]
                arrivals.append((block, pltpu.make_async_copy(source, target, in_sems.at[len(arrivals)])))
                arrivals[-1][1].start()

        def read_first(block):
            early, late = block <= geo.attention_blocks, block >= geo.vector_blocks
            return early or late if isinstance(block, int) else early | late

        in_waves(arrivals, read_first, True, lambda copy: copy.wait())

        def spans(matrix, low, high):
            for first, last, places in geo.runs[matrix]:
                start, stop = max(first, low), min(last, high)
                if start < stop:
                    yield start, stop, places

        def ref_rows(place, column, start, stop):
            block, first, last, base = place
            at = base + column * (last - first) + start - first
            return store.at[block, pl.ds(aligned(at), stop - start), :]

        def load(matrix, column, low=0, high=None):
            parts = []
            for start, stop, places in spans(matrix, low, high or up_to(MATRICES[matrix][0], ROUND)):
                value = ref_rows(places[0], column, start, stop)[...]
                for place in places[1:]:
                    value = value + ref_rows(place, column, start, stop)[...]
                parts.append(value)
            return parts[0] if len(parts) == 1 else jnp.concatenate(parts, axis=0)

        def load_wide(matrix, column, wide, low=0, high=None):
            return jnp.concatenate([load(matrix, column + i, low, high) for i in range(wide)], axis=1)

        def save(matrix, column, value, low=0):
            for start, stop, places in spans(matrix, low, low + value.shape[0]):
                for place in places:
                    ref_rows(place, column, start, stop)[...] = value[start - low : stop - low, :]

        def save_wide(matrix, column, value, low=0):
            value = value.astype(BF16)
            for i in range(value.shape[1] // LANES):
                save(matrix, column + i, value[:, i * LANES : (i + 1) * LANES], low)

        def vec(row, wide):
            return jnp.concatenate([vecs[pl.ds(row + i, 1), :] for i in range(wide)], axis=1)

        def vec_grad(row, value):
            sums = jnp.sum(value, axis=0, keepdims=True)
            for i in range(sums.shape[1] // LANES):
                vec_grads[pl.ds(row + i, 1), :] = sums[:, i * LANES : (i + 1) * LANES]

        vecs[...] = load(VEC, 0).astype(F32)
        vec_grads[...] = jnp.zeros((VEC_ROWS, LANES), F32)

        sines = sinusoid_ref[...]
        time_pre = nn(sines, load_wide(TIME_IN, 0, 4)) + vec(V_TIME_IN, 4)
        time_gate = 1.0 / (1.0 + jnp.exp(-time_pre))
        time_act = (time_pre * time_gate).astype(BF16)
        time_emb = nn(time_act, load_wide(TIME_OUT, 0, 6)) + vec(V_TIME_OUT, 6)
        for seq in range(seqs):
            span = pl.ds(seq * L, L)
            value = tokens_ref[span, :].astype(F32) + time_emb[seq : seq + 1, :]
            rows_zero[span, :] = value
            rows_low[span, :] = value.astype(BF16)

        for tile in range(9):
            value = nn(rows_low[...], load_wide(QKV, 2 * tile, 2))
            if tile < 3:
                value = value + vec(V_Q + 2 * tile, 2)
            if tile >= 6:
                value = value + vec(V_V + 2 * (tile - 6), 2)
            qkv[:, tile * 256 : (tile + 1) * 256] = value.astype(BF16)

        first_head = lax.broadcasted_iota(jnp.int32, (L, LANES), 1) < HEAD_DIM

        def split_heads(value):
            zero = jnp.zeros_like(value)
            return jnp.concatenate([jnp.where(first_head, value, zero), jnp.where(first_head, zero, value)], axis=0)

        def both(value):
            return jnp.concatenate([jnp.broadcast_to(item, (L, L)) for item in value], axis=1)

        def pair_at(seq, pair, part):
            return qkv[pl.ds(seq * L, L), pl.ds(part * D + pair * LANES, LANES)]

        key = lax.broadcasted_iota(jnp.int32, (L, 2 * L), 1) % L
        for seq in range(seqs):
            valid = key < lengths_ref[seq]
            for pair in range(pairs):
                scores = nt(pair_at(seq, pair, 0), split_heads(pair_at(seq, pair, 1))) * scale
                scores = jnp.where(valid, scores, -1e30)
                top = both([jnp.max(scores[:, i * L : (i + 1) * L], axis=1, keepdims=True) for i in range(2)])
                power = jnp.exp(scores - top)
                sums = [jnp.sum(power[:, i * L : (i + 1) * L], axis=1, keepdims=True) for i in range(2)]
                weight = power * both([1.0 / item for item in sums])
                probs[seq * pairs + pair] = weight
                value = nn(weight.astype(BF16), split_heads(pair_at(seq, pair, 2)))
                context[pl.ds(seq * L, L), pl.ds(pair * LANES, LANES)] = value.astype(BF16)

        for tile in range(3):
            cols = pl.ds(tile * 256, 256)
            value = nn(context[...], load_wide(OUT, 2 * tile, 2)) + vec(V_OUT + 2 * tile, 2)
            total[:, cols] = rows_zero[:, cols] + value
        hat, inverse_one = norm_parts(total[...])
        hat_one[...] = hat
        gain_one = vec(V_GAIN1, 6)
        value = hat * gain_one + vec(V_SHIFT1, 6)
        hidden[...] = value
        hidden_low[...] = value.astype(BF16)
        hidden_t[...] = value.astype(BF16).T

        in_waves(arrivals, read_first, False, lambda copy: copy.wait())

        def up_step(tile, carry):
            pre = nn(hidden_low[...], load_wide(UP, 2 * tile, 2)) + vec(V_UP + 2 * tile, 2)
            below = 0.5 * (1.0 + lax.erf(pre * (0.5**0.5)))
            cols = pl.ds(aligned(tile * 256, 256), 256)
            act[:, cols] = (pre * below).astype(BF16)
            slope[:, cols] = below + pre * (jnp.exp(-0.5 * pre * pre) * (1.0 / math.sqrt(2.0 * math.pi)))
            return carry

        lax.fori_loop(0, 12, up_step, 0, unroll=2)
        for tile in range(3):
            cols = pl.ds(tile * 256, 256)
            value = nn(act[...], load_wide(DOWN, 2 * tile, 2)) + vec(V_DOWN + 2 * tile, 2)
            total[:, cols] = hidden[:, cols] + value

        hat, inverse = norm_parts(total[...])
        gain_two = vec(V_GAIN2, 6)
        output_ref[...] = (hat * gain_two + vec(V_SHIFT2, 6)).astype(BF16)
        d_result = cotangent_ref[...].astype(F32)
        vec_grad(V_GAIN2, d_result * hat)
        vec_grad(V_SHIFT2, d_result)
        value = norm_back(d_result * gain_two, hat, inverse)
        d_hidden[...] = value
        d_down = value.astype(BF16)
        vec_grad(V_DOWN, d_down.astype(F32))

        for tile in range(12):
            low, high = tile * 256, (tile + 1) * 256
            cols = pl.ds(low, 256)
            d_act = nt(d_down, load_wide(DOWN, 0, 6, low, high))
            save_wide(DOWN, 0, nn(act[:, cols].T, d_down), low)
            d_up = (d_act * slope[:, cols]).astype(BF16)
            vec_grad(V_UP + 2 * tile, d_up.astype(F32))
            d_hidden[...] += nt(d_up, load_wide(UP, 2 * tile, 2))
            save_wide(UP, 2 * tile, nn(hidden_t[...], d_up))

        departures, near_refs = [], []
        for near, ref, (blocks, at, length) in zip(near_grads, grad_refs, grad_parts(index)):
            if near:
                near_refs.append((ref, blocks[0]))
                continue
            for i, block in enumerate(range(geo.shards) if blocks is None else blocks):
                source = store.at[block, pl.ds(at, length), :]
                departures.append((block, pltpu.make_async_copy(source, ref.at[i], out_sems.at[len(departures)])))

        def done_first(block):
            late, early = block > geo.attention_blocks, block < geo.vector_blocks
            return early and late if isinstance(block, int) else early & late

        in_waves(departures, done_first, True, lambda copy: copy.start())

        d_out = d_hidden[...]
        hat = hat_one[...]
        vec_grad(V_GAIN1, d_out * hat)
        vec_grad(V_SHIFT1, d_out)
        value = norm_back(d_out * gain_one, hat, inverse_one)
        total[...] = value
        d_attn = value.astype(BF16)
        vec_grad(V_OUT, d_attn.astype(F32))
        d_context = nt(d_attn, load_wide(OUT, 0, 6)).astype(BF16)
        context_t = context[...].T
        for tile in range(3):
            save_wide(OUT, 2 * tile, nn(context_t, d_attn[:, tile * 256 : (tile + 1) * 256]))
        context[...] = d_context

        for seq in range(seqs):
            span = pl.ds(seq * L, L)
            for pair in range(pairs):
                weight = probs[seq * pairs + pair]
                d_pair = context[span, pl.ds(pair * LANES, LANES)]
                query, keys = pair_at(seq, pair, 0), pair_at(seq, pair, 1)
                d_weight = nt(d_pair, split_heads(pair_at(seq, pair, 2)))
                mixed = weight * d_weight
                delta = both([jnp.sum(mixed[:, i * L : (i + 1) * L], axis=1, keepdims=True) for i in range(2)])
                d_scores = (weight * (d_weight - delta)).astype(BF16)
                d_query = nn(d_scores, split_heads(keys)) * scale
                stacked = nn(d_scores.T, query)
                d_key = jnp.where(first_head, stacked[:L], stacked[L:]) * scale
                stacked = nn(weight.astype(BF16).T, d_pair)
                d_value = jnp.where(first_head, stacked[:L], stacked[L:])
                for part, item in enumerate((d_query, d_key, d_value)):
                    d_qkv[span, pl.ds(part * D + pair * LANES, LANES)] = item.astype(BF16)

        rows_t = rows_low[...].T
        for tile in range(9):
            value = d_qkv[:, tile * 256 : (tile + 1) * 256]
            if tile < 3:
                vec_grad(V_Q + 2 * tile, value.astype(F32))
            if tile >= 6:
                vec_grad(V_V + 2 * (tile - 6), value.astype(F32))
            total[...] += nt(value, load_wide(QKV, 2 * tile, 2))
            save_wide(QKV, 2 * tile, nn(rows_t, value))
        d_rows = total[...]
        token_grad_ref[...] = d_rows

        d_time = [jnp.sum(d_rows[seq * L : (seq + 1) * L], axis=0, keepdims=True) for seq in range(seqs)]
        d_time = jnp.concatenate(d_time + [jnp.zeros((sines.shape[0] - seqs, D), F32)], axis=0).astype(BF16)
        vec_grad(V_TIME_OUT, d_time.astype(F32))
        d_time_act = nt(d_time, load_wide(TIME_OUT, 0, 6))
        save_wide(TIME_OUT, 0, nn(time_act.T, d_time))
        d_time_pre = (d_time_act * (time_gate * (1.0 + time_pre * (1.0 - time_gate)))).astype(BF16)
        vec_grad(V_TIME_IN, d_time_pre.astype(F32))
        save_wide(TIME_IN, 0, nn(sines.T, d_time_pre))
        save(VEC, 0, vec_grads[...].astype(BF16))

        in_waves(departures, done_first, False, lambda copy: copy.start())
        for ref, block in near_refs:
            ref[0] = store[block]
        in_waves(departures, done_first, True, lambda copy: copy.wait())
        in_waves(departures, done_first, False, lambda copy: copy.wait())

    whole = pl.BlockSpec(memory_space=pltpu.VMEM)
    return pl.pallas_call(
        kernel,
        in_specs=[pl.BlockSpec(memory_space=pltpu.SMEM)] * 2
        + [whole] * 3
        + [pl.BlockSpec(memory_space=pl.ANY) if item.size >= geo.rows * LANES else whole for item in pieces],
        out_specs=[whole] * 2 + [whole if near else pl.BlockSpec(memory_space=pltpu.HBM) for near in near_grads],
        out_shape=[
            jax.ShapeDtypeStruct((rows, D), BF16),
            jax.ShapeDtypeStruct((rows, D), F32),
        ]
        + [jax.ShapeDtypeStruct(shape, BF16) for shape in grad_shapes],
        scratch_shapes=[
            pltpu.VMEM((geo.shards, geo.rows, LANES), BF16),
            pltpu.VMEM((VEC_ROWS, LANES), F32),
            pltpu.VMEM((VEC_ROWS, LANES), F32),
            pltpu.VMEM((rows, D), F32),
            pltpu.VMEM((rows, D), BF16),
            pltpu.VMEM((rows, 3 * D), BF16),
            pltpu.VMEM((seqs * pairs, L, 2 * L), F32),
            pltpu.VMEM((rows, D), BF16),
            pltpu.VMEM((rows, D), F32),
            pltpu.VMEM((rows, D), F32),
            pltpu.VMEM((rows, D), BF16),
            pltpu.VMEM((D, rows), BF16),
            pltpu.VMEM((rows, FF), BF16),
            pltpu.VMEM((rows, FF), F32),
            pltpu.VMEM((rows, D), F32),
            pltpu.VMEM((rows, D), F32),
            pltpu.VMEM((rows, 3 * D), BF16),
            pltpu.SemaphoreType.DMA((in_count,)),
            pltpu.SemaphoreType.DMA((out_count,)),
        ],
        compiler_params=pltpu.CompilerParams(vmem_limit_bytes=20 * 2**20 + geo.shards * geo.rows * LANES * 2),
        name="model_step",
    )(where, lengths, tokens, cotangent, sinusoid, *pieces)


def neighbor_quarters(index, replica):
    core = index % 2
    return replica, replica ^ (1 + core), replica ^ (2 - core), replica ^ 3


def small_step(name, body, scalars, inputs, shapes, after):
    def kernel(*refs):
        first, last = len(scalars), len(scalars) + len(inputs)
        body(refs[:first], refs[first:last], refs[last + len(after) : -1])
        refs[-1][...] = jnp.zeros(TOKEN, F32)

    whole = pl.BlockSpec(memory_space=pltpu.VMEM)
    return pl.pallas_call(
        kernel,
        in_specs=[pl.BlockSpec(memory_space=pltpu.SMEM)] * len(scalars)
        + [whole] * len(inputs)
        + [pl.BlockSpec(memory_space=pl.ANY)] * len(after),
        out_specs=[whole] * (len(shapes) + 1),
        out_shape=[jax.ShapeDtypeStruct(shape, BF16) for shape in shapes] + [jax.ShapeDtypeStruct(TOKEN, F32)],
        compiler_params=pltpu.CompilerParams(vmem_limit_bytes=12 * 2**20),
        name=name,
    )(*scalars, *inputs, *after)


def stack_up(after, *groups):
    def body(scalars, inputs, outs):
        inputs = list(inputs)
        for group, out in zip(groups, outs):
            at = 0
            for item in group:
                out[pl.ds(at, item.shape[0]), :] = inputs.pop(0)[...]
                at += item.shape[0]

    items = [item for group in groups for item in group]
    shapes = [(sum(item.shape[0] for item in group), LANES) for group in groups]
    return small_step("stack_up", body, [], items, shapes, after)


def reduce_step(geo, where, after, cores=None, pair=None, items=None, head=None, tails=None, halves=False):
    size = geo.quarter
    inputs, shapes = [], []
    if cores is not None:
        inputs += cores + [tails] * (tails is not None)
        shapes += [(2, head or size, LANES)] * 2 + [(4 * (size - (head or 0)), LANES)] * (head is not None)
    if pair is not None:
        inputs += pair
        rows = pair[0].shape[1]
        shapes += [(rows // 2, LANES)] * 4 if halves else [(rows, LANES)] * 2
    if items is not None:
        inputs += items
        rows = items[0].shape[0]
        shapes += [(rows // 2, LANES)] * 2 if halves else [(rows, LANES)]

    def body(scalars, inputs, outs):
        inputs, outs = list(inputs), list(outs)

        def save(value):
            start = 0
            while start < value.shape[0]:
                out = outs.pop(0)
                out[...] = value[start : start + out.shape[0], :].astype(BF16)
                start += out.shape[0]

        if cores is not None:
            keep, got = inputs[:2]
            for i, quarter in enumerate(neighbor_quarters(scalars[0][0], scalars[0][1])):
                span = pl.ds(aligned(quarter * size), head or size)
                value = keep[span, :].astype(F32) + got[span, :].astype(F32)
                if tails is not None:
                    more = inputs[2].shape[0] // 4
                    tail = inputs[2][pl.ds(aligned(quarter * more), more), :].astype(F32)
                    value = jnp.concatenate([value[: size - more], value[size - more :] + tail], axis=0)
                outs[i // 2][i % 2] = value.astype(BF16)
            if head is not None:
                more = size - head
                for i in range(4):
                    span = pl.ds(i * size + head, more)
                    value = keep[span, :].astype(F32) + got[span, :].astype(F32)
                    outs[2][pl.ds(i * more, more), :] = value.astype(BF16)
            inputs = inputs[2 + (tails is not None) :]
            del outs[: 2 + (head is not None)]
        if pair is not None:
            near, got = inputs[:2]
            for i in range(2):
                save(near[i].astype(F32) + got[i].astype(F32))
            inputs = inputs[2:]
        if items is not None:
            edges = sorted({0} | {ref.shape[0] for ref in inputs})
            values = []
            for low, high in zip(edges, edges[1:]):
                parts = [ref[pl.ds(low, high - low), :].astype(F32) for ref in inputs if ref.shape[0] > low]
                values.append(sum(parts[1:], parts[0]))
            save(values[0] if len(values) == 1 else jnp.concatenate(values, axis=0))

    return small_step("reduce_step", body, [where], inputs, shapes, after)


def ring_order(size):
    return list(range(0, size, 2))[:1] + list(range(1, size, 2)) + list(range(size - 2, 0, -2))


def select(value, choices):
    out = jnp.int32(choices[0])
    for i, choice in enumerate(choices[1:], 1):
        out = jnp.where(value == i, choice, out)
    return out


def make_local(dp, fsdp):
    direct_links = dp == 4 and fsdp == 8
    chips = fsdp // 2
    order = ring_order(chips)
    before = [order[order.index(chip) - 1] for chip in range(chips)]

    def chip_before(chip, hops):
        table = list(range(chips))
        for _ in range(hops):
            table = [before[item] for item in table]
        return select(chip, table)

    def permute(value, axes, target):
        pairs = []
        for replica in range(dp):
            for index in range(fsdp):
                pairs.append((replica * fsdp + index, target(replica, index)))
        return lax.ppermute(value, axes, pairs)

    def core_swap(value):
        return lax.ppermute(value, "fsdp", [(index, index ^ 1) for index in range(fsdp)])

    def ring_hop(value, hops=1):
        pairs = []
        for place, chip in enumerate(order):
            target = order[(place + hops) % chips]
            pairs += [(chip * 2 + core, target * 2 + core) for core in range(2)]
        return lax.ppermute(value, "fsdp", pairs)

    def first_way(value):
        return permute(value, ("dp", "fsdp"), lambda r, i: (r ^ (1 + i % 2)) * fsdp + i)

    def second_way(value):
        return permute(value, ("dp", "fsdp"), lambda r, i: (r ^ (2 - i % 2)) * fsdp + i)

    def local(tokens, lengths, timesteps, cotangent, params, moment_one, moment_two):
        geo = Geometry(params.shape[0] * fsdp, fsdp)
        where = jnp.stack([lax.axis_index("fsdp"), lax.axis_index("dp")]).astype(jnp.int32)
        seqs = tokens.shape[0]

        half_freq = TFREQ // 2
        frequencies = jnp.exp(-math.log(10000.0) * jnp.arange(half_freq, dtype=F32) / half_freq)
        angles = timesteps.astype(F32)[:, None] * frequencies[None, :]
        sinusoid = jnp.concatenate([jnp.cos(angles), jnp.sin(angles)], axis=1).astype(BF16)
        sinusoid = jnp.pad(sinusoid, ((0, up_to(seqs, ROUND) - seqs), (0, 0)))

        block, quarter = pack_block(geo, params, where)

        def block_of(hops, other=0):
            return lambda index: chip_before(index // 2, hops) * 2 + (index % 2 ^ other)

        if direct_links:
            swapped = core_swap(block)
            pieces = [block, swapped]

            def swap(item):
                other = core_swap(item)
                pieces.extend([item, other])
                return other

            near_1, token = stack_up([], [ring_hop(quarter)])
            hop, one_1, two_1 = ring_hop(near_1), first_way(near_1), second_way(near_1)
            near_2, pair_1, token = stack_up([token, swapped, swap(near_1), two_1], [hop], [hop, one_1])
            hop, one_2, far_1 = ring_hop(near_2), first_way(near_2), second_way(pair_1)
            near_3, pair_2, token = stack_up([token, swap(two_1), swap(pair_1)], [hop], [hop, one_2])
            one_3, far_2 = first_way(near_3), second_way(pair_2)
            one_3, token = stack_up([token, swap(pair_2)], [one_3])
            three_3 = second_way(one_3)
            for item in (far_1, one_3, far_2, three_3):
                swap(item)

            def weight_places(index, replica):
                size = geo.quarter
                groups = (
                    ((1, 0),),
                    ((1, 2),),
                    ((2, 0), (1, 1)),
                    ((3, 0), (2, 1)),
                    ((2, 2), (1, 3)),
                    ((3, 1),),
                    ((3, 2), (2, 3)),
                    ((3, 3),),
                )
                places = [[(block_of(0, other)(index), 0, geo.rows, 0)] for other in range(2)]
                for group in groups:
                    for other in range(2):
                        quarters = neighbor_quarters(index ^ other, replica)
                        places.append([
                            (block_of(hops, other)(index), i * size, size, quarters[quarter] * size)
                            for i, (hops, quarter) in enumerate(group)
                        ])
                return places

            def grad_parts(index):
                kept = [block_of(hops)(index) for hops in range(1, chips + 1)]
                sent = [block_of(hops, 1)(index) for hops in range(1, chips + 1)]
                return [([block], 0, geo.rows) for block in kept + sent]

        else:
            pieces = [lax.all_gather(block, "fsdp", axis=0)]

            def weight_places(index, replica):
                return [0]

            def grad_parts(index):
                return [(None, 0, geo.rows)]

        output, token_grad, *grads = model_step(
            geo,
            tokens.reshape(seqs * L, D),
            cotangent.reshape(seqs * L, D),
            lengths,
            sinusoid,
            where,
            pieces,
            weight_places,
            grad_parts,
        )

        if direct_links:
            grads = [item[0] for item in grads]
            cores = [[grads[hops], core_swap(grads[chips + hops])] for hops in range(chips)]
            near_1, far_1, tails, token = reduce_step(geo, where, [], cores=cores[0], head=geo.head)
            far_1, tails = second_way(far_1), ring_hop(tails, -1)
            near_2, far_2, token = reduce_step(geo, where, [token], cores=cores[1])
            far_2 = second_way(far_2)
            near_3, far_3, own_1, next_1, token = reduce_step(geo, where, [token], cores=cores[2], pair=[near_1, far_1])
            next_1, far_3 = first_way(next_1), second_way(far_3)
            quarter, token = reduce_step(geo, where, [token], items=[own_1, next_1])
            passed = ring_hop(quarter)
            near_4, far_4, own_2, next_2, token = reduce_step(
                geo, where, [token], cores=cores[3], pair=[near_2, far_2], tails=tails
            )
            next_2, far_4 = first_way(next_2), second_way(far_4)
            own_3, next_3, token = reduce_step(geo, where, [token], pair=[near_3, far_3])
            next_3 = first_way(next_3)
            quarter, token = reduce_step(geo, where, [token], items=[own_2, next_2, passed])
            passed = ring_hop(quarter)
            own_a, own_b, next_a, next_b, token = reduce_step(geo, where, [token], pair=[near_4, far_4], halves=True)
            next_a, next_b = first_way(next_a), first_way(next_b)
            passed_a, passed_b, token = reduce_step(geo, where, [token], items=[own_3, next_3, passed], halves=True)
            passed_a, passed_b = ring_hop(passed_a), ring_hop(passed_b)
            half_a, token = reduce_step(geo, where, [token], items=[own_a, next_a, passed_a])
            one_a, two_a = first_way(half_a), second_way(half_a)
            half_b, token = reduce_step(geo, where, [token], items=[own_b, next_b, passed_b])
            one_b, two_b = first_way(half_b), second_way(half_b)
            pieces = [half_a, half_b, one_a, one_b, two_a, two_b, second_way(one_a), second_way(one_b)]

            def piece_places(index, replica):
                half = geo.quarter // 2
                return [
                    (2 * i + j, 0, half, item * geo.quarter + j * half)
                    for i, item in enumerate(neighbor_quarters(index, replica))
                    for j in range(2)
                ]

        else:
            mine = lax.psum_scatter(grads[0], "fsdp", scatter_dimension=0)
            pieces = [lax.psum(mine, "dp")]

            def piece_places(index, replica):
                return [(0, 0, geo.rows, 0)]

        new_params, new_one, new_two = optimizer_step(
            geo, params, moment_one, moment_two, where, pieces, piece_places
        )
        return (
            output.reshape(tokens.shape),
            token_grad.reshape(tokens.shape),
            new_params,
            new_one,
            new_two,
        )

    return local


def solution(mesh):
    batch = P(("dp", "fsdp"))
    rows = P(("dp", "fsdp"), None, None)
    flat = P("fsdp")
    return jax.shard_map(
        make_local(mesh.shape["dp"], mesh.shape["fsdp"]),
        mesh=mesh,
        in_specs=(rows, batch, batch, rows, flat, flat, flat),
        out_specs=(rows, rows, flat, flat, flat),
        check_vma=False,
    )
```
